512 devices in a mesh: row: 32 (over y, x), col: 16 (over z, core).
Axes of the slice: x: 4, y: 8, z: 8, core: 2. Of those that a mesh axis runs over, the one named last changes fastest.
Arguments:
- rhs: bfloat16 [2, 4096, 256], P(None, 'row'), may hold values from -6 to 6
- lower_factor: bfloat16 [2, 4096, 4096], P(None, 'row', 'col'), may hold values from -2 to 2
- upper_factor: bfloat16 [2, 4096, 4096], P(None, 'row', 'col'), may hold values from -2 to 2
- lower_rest: bfloat16 [2, 12288, 4096], P(None, 'row', 'col'), may hold values from -0.09375 to 0.09375
- upper_rest: bfloat16 [2, 4096, 12288], P(None, 'row', 'col'), may hold values from -0.0546875 to 0.0546875
- rest_solution: bfloat16 [2, 256, 12288], P(None, 'row', 'col'), may hold values from -6 to 6
- rest_rhs: bfloat16 [12288, 2, 256], P(('row', 'col')), may hold values from -6 to 6
Outputs:
- solution: bfloat16 [2, 4096, 256], P(None, 'col')
- rest_out: bfloat16 [12288, 2, 256], P(('row', 'col'))
The draws below stay inside these ranges and needn't reach their ends.
All inputs are finite; a program needn't handle non-finite values.
Results may differ from the reference program's by a relative error of at most 0.04.
Values may be sent and summed in bfloat16 or wider, within the bound.
No kernel may reach another device: no remote copies, remote signals or barrier semaphores. Data moves between devices by JAX's collectives and lax.ppermute only.
A program may use at most 64 MiB of HBM per device.

```python
import math
import jax
import jax.numpy as jnp
from jax import lax

N = 4096
NB = 1024
R = 256
M = 12288
TILE_ROWS = 128


def factor_draw(key, direction):
    first_key, second_key, third_key = jax.random.split(key, 3)
    row_block = (jnp.arange(N) // NB)[:, None]
    col_block = (jnp.arange(N) // NB)[None, :]
    outside = jax.random.normal(first_key, (2, N, N), jnp.float32) * (1.0 / math.sqrt(N))
    inside = jax.random.normal(second_key, (2, N, N), jnp.float32) * (0.5 / math.sqrt(NB))
    scales = jax.random.uniform(third_key, (N,), jnp.float32, 0.7, 1.4)
    identity = jnp.eye(N, dtype=jnp.float32) * scales[:, None]
    diagonal = inside + jnp.stack([identity, jnp.zeros_like(identity)])
    strict = direction * (row_block - col_block) > 0
    drawn = jnp.where(row_block == col_block, diagonal, jnp.where(strict, outside, 0.0))
    return drawn.astype(jnp.bfloat16)


def draw_lower_factor(key, part):
    key = jax.random.fold_in(key, 11)
    return factor_draw(key, 1.0)


def draw_upper_factor(key, part):
    key = jax.random.fold_in(key, 23)
    return factor_draw(key, -1.0)


def block_levels(rng, shape, cuts, smallest, top_value):
    loudness = 1.0
    for dim, blocks in cuts:
        draws = jax.random.uniform(jax.random.fold_in(jax.random.fold_in(rng, 6), dim), (blocks,), jnp.float32, smallest / len(cuts), top_value / len(cuts))
        loudness = loudness * jnp.repeat(jnp.exp(draws), shape[dim] // blocks).reshape((-1,) + (1,) * (len(shape) - 1 - dim))
    return loudness


def bell_draw(rng, shape, width, limit, cuts=(), held_as=jnp.bfloat16):
    result = width * jax.random.normal(rng, shape, jnp.float32)
    if cuts:
        result = result * block_levels(rng, shape, cuts, -0.22, 0.18)
    return jnp.clip(result, -limit, limit).astype(held_as)


def setup_inputs(seed: int = 0) -> dict:
    arg_keys = jax.random.split(jax.random.key(seed), 8)
    rhs = bell_draw(arg_keys[0], (2, N, R), 1.0, 6.0, ((1, 32),))
    lower_factor = draw_lower_factor(jax.random.fold_in(arg_keys[7], 71), 0)
    upper_factor = draw_upper_factor(jax.random.fold_in(arg_keys[7], 71), 0)
    lower_rest = bell_draw(arg_keys[3], (2, M, N), N ** -0.5, 0.09375, ((1, 32), (2, 16)))
    upper_rest = bell_draw(arg_keys[4], (2, N, M), M ** -0.5, 0.0546875, ((1, 32), (2, 16)))
    rest_solution = bell_draw(arg_keys[5], (2, R, M), 1.0, 6.0, ((1, 32), (2, 16)))
    rest_rhs = bell_draw(arg_keys[6], (M, 2, R), 1.0, 6.0, ((0, 512),))
    return {"rhs": rhs, "lower_factor": lower_factor, "upper_factor": upper_factor, "lower_rest": lower_rest, "upper_rest": upper_rest, "rest_solution": rest_solution, "rest_rhs": rest_rhs}


def complex_product(left, right):
    def single(first, second):
        return jnp.dot(first, second, preferred_element_type=jnp.float32)
    return jnp.stack([single(left[0], right[0]) - single(left[1], right[1]),
                      single(left[0], right[1]) + single(left[1], right[0])])


def complex_transposed(left, right):
    def single(first, second):
        return jnp.dot(first.T, second, preferred_element_type=jnp.float32)
    return jnp.stack([single(left[0], right[0]) - single(left[1], right[1]),
                      single(left[0], right[1]) + single(left[1], right[0])])


def block_solve(diagonal, residual):
    summed = jnp.zeros((2, NB, residual.shape[2]), jnp.float32)
    for group in range(NB // TILE_ROWS):
        first = group * TILE_ROWS
        piece = complex_transposed(diagonal[:, first:first + TILE_ROWS, :], residual[:, first:first + TILE_ROWS, :])
        piece = lax.optimization_barrier(piece.astype(jnp.bfloat16))
        summed = summed + piece.astype(jnp.float32)
    return summed.astype(jnp.bfloat16)


def reference(rhs, lower_factor, upper_factor, lower_rest, upper_rest, rest_solution, rest_rhs):
    block_count = N // NB
    solved_blocks = []
    for k in range(block_count):
        first = k * NB
        if k == 0:
            residual = rhs[:, 0:NB, :]
        else:
            earlier = jnp.concatenate(solved_blocks, axis=1)
            reduced = complex_product(lower_factor[:, first:first + NB, 0:first], earlier)
            residual = (rhs[:, first:first + NB, :].astype(jnp.float32) - reduced).astype(jnp.bfloat16)
        solved_blocks.append(block_solve(lower_factor[:, first:first + NB, first:first + NB], residual))
    forward = jnp.concatenate(solved_blocks, axis=1)
    update = jnp.transpose(complex_product(lower_rest, forward), (1, 0, 2))
    rest_out = (rest_rhs.astype(jnp.float32) - update).astype(jnp.bfloat16)
    trailing = complex_product(upper_rest, jnp.transpose(rest_solution, (0, 2, 1)))
    backward_blocks = [None] * block_count
    for k in reversed(range(block_count)):
        first = k * NB
        reduced = trailing[:, first:first + NB, :]
        if k < block_count - 1:
            after_blocks = jnp.concatenate(backward_blocks[k + 1:], axis=1)
            reduced = reduced + complex_product(upper_factor[:, first:first + NB, first + NB:], after_blocks)
        residual = (forward[:, first:first + NB, :].astype(jnp.float32) - reduced).astype(jnp.bfloat16)
        backward_blocks[k] = block_solve(upper_factor[:, first:first + NB, first:first + NB], residual)
    solution = jnp.concatenate(backward_blocks, axis=1)
    return solution, rest_out
```

```python
import jax
import jax.numpy as jnp
from jax import lax
from jax.sharding import PartitionSpec as P

N = 4096
NB = 1024
BLOCKS = N // NB


def nt(left, right):
    return lax.dot_general(left, right, (((1,), (1,)), ((), ())), preferred_element_type=jnp.float32)


def nn(left, right):
    return jnp.dot(left, right, preferred_element_type=jnp.float32)


def pair_groups(first, second, width):
    others = [k for k in range(BLOCKS) if k not in (first, second)]

    def members(k):
        return [k * width + i for i in range(width)]

    return [members(first) + members(second), members(others[0]) + members(others[1])]


def exchange(value, axis, groups=None):
    return lax.all_to_all(value, axis, 0, 0, axis_index_groups=groups)


def repeat_for(value, count):
    return jnp.broadcast_to(value[None], (count,) + value.shape)


def solve(residual, stored, half):
    width = stored.shape[1] // 2
    product = nn(residual, stored)
    real = product[:half, :width] - product[half:, width:]
    imag = product[:half, width:] + product[half:, :width]
    return jnp.concatenate([real, imag], axis=0)


def spread(solved, panel, half):
    real, imag = solved[:half], solved[half:]
    left = jnp.concatenate(
        [jnp.concatenate([real, -imag], axis=1), jnp.concatenate([imag, real], axis=1)], axis=0
    )
    return nt(left, panel)


def per_device(rhs, lower_factor, upper_factor, lower_rest, upper_rest, rest_solution, rest_rhs):
    rows, cols = lax.axis_size("row"), lax.axis_size("col")
    row_index = lax.axis_index("row")
    col_index = lax.axis_index("col")
    tile_rows = lower_factor.shape[1]
    tile_cols = lower_factor.shape[2]
    sources = rhs.shape[2]
    half = sources // rows
    both = 2 * half
    row_width = rows // BLOCKS
    width = cols // BLOCKS
    row_block = row_index // row_width
    col_block = col_index // width
    place = col_index % width
    bf16, f32 = jnp.bfloat16, jnp.float32

    tile = jnp.where(row_block >= col_block, lower_factor, upper_factor)
    tile = jnp.concatenate([tile[0], tile[1]], axis=1)
    panel = lax.all_gather(tile, "row", axis=0, tiled=True)

    quarter = tile_rows // BLOCKS
    upper = jnp.concatenate([upper_factor[0], upper_factor[1]], axis=1)
    same = [[j * row_width + i for j in range(BLOCKS)] for i in range(row_width)]
    quarters = exchange(upper.reshape(BLOCKS, quarter, 2 * tile_cols), "row", same)
    mine = lax.dynamic_index_in_dim(quarters, col_block, 0, keepdims=False)
    upper_diagonal = lax.all_gather(mine, "row", axis=0, tiled=True)
    upper_diagonal = upper_diagonal.reshape(BLOCKS, row_width, quarter, 2 * tile_cols)
    upper_diagonal = jnp.transpose(upper_diagonal, (1, 0, 2, 3)).reshape(NB, 2 * tile_cols)

    by_source = jnp.transpose(rhs, (0, 2, 1)).reshape(2, rows, half, tile_rows)
    by_source = jnp.transpose(by_source, (1, 0, 2, 3))
    sent = jnp.concatenate([by_source, repeat_for(rest_solution, rows)], axis=3)
    got = exchange(sent, "row")
    own_rhs = lax.dynamic_slice_in_dim(got[..., :tile_rows], col_block * row_width, row_width, 0)
    own_rhs = jnp.transpose(own_rhs, (1, 2, 0, 3)).reshape(both, NB).astype(f32)

    rest = jnp.transpose(got[..., tile_rows:], (1, 0, 2, 3)).reshape(2, sources, -1)
    real = nt(rest[0], upper_rest[0]) - nt(rest[1], upper_rest[1])
    imag = nt(rest[0], upper_rest[1]) + nt(rest[1], upper_rest[0])
    trailing = jnp.stack([real, imag]).astype(bf16).reshape(2, rows, half, tile_rows)
    trailing = exchange(jnp.transpose(trailing, (1, 0, 2, 3)), "row")
    per_col = rows // cols
    trailing = exchange(trailing.reshape(cols, per_col, 2, half, tile_rows), "col")
    trailing = jnp.sum(trailing.astype(f32), axis=0)
    trailing = jnp.transpose(trailing, (1, 2, 0, 3)).reshape(both, tile_cols)

    def step(solved, carried, part, order, this, following):
        count = len(order)
        products = spread(solved, part, half).reshape(both, count, width, tile_cols)
        if carried is not None:
            at_place = (lax.iota(jnp.int32, width) == place)[None, None, :, None]
            products = products + jnp.where(at_place, carried[:, :, None, :], 0.0)
        products = products.astype(bf16)
        near = repeat_for(products[:, order[0]].reshape(both, NB), width)
        pieces = [near]
        for later in order[1:]:
            pieces.append(jnp.transpose(products[:, later], (1, 0, 2)))
        payload = jnp.concatenate(pieces, axis=2)
        payload = jnp.concatenate([payload, payload], axis=0)
        arrived = exchange(payload, "col", pair_groups(this, following, width))
        arrived = jnp.sum(arrived[:width].astype(f32), axis=0)
        return arrived[:, :NB], arrived[:, NB:].reshape(both, count - 1, tile_cols)

    forward = jnp.zeros((both, tile_cols), bf16)
    reduced = jnp.zeros((both, NB), f32)
    carried = None
    for k in range(BLOCKS):
        holder = col_block == k
        residual = (own_rhs - reduced).astype(bf16)
        value = solve(residual, panel[k * NB : (k + 1) * NB], half).astype(bf16)
        forward = jnp.where(holder, value, forward)
        if k < BLOCKS - 1:
            solved = jnp.where(holder, value, jnp.zeros_like(value))
            count = BLOCKS - 1 - k
            reduced, carried = step(
                solved, carried, panel[(k + 1) * NB :], list(range(count)), k, k + 1
            )
            carried = jnp.where(col_block == k + 1, carried, 0.0)

    forward_all = lax.all_gather(forward, "row", axis=0, tiled=True)

    forward_all = jnp.transpose(forward_all.reshape(rows, 2, half, tile_cols), (1, 0, 2, 3))
    forward_all = forward_all.reshape(2, sources, tile_cols)
    real = nt(lower_rest[0], forward_all[0]) - nt(lower_rest[1], forward_all[1])
    imag = nt(lower_rest[0], forward_all[1]) + nt(lower_rest[1], forward_all[0])
    update = jnp.stack([real, imag], axis=1).astype(bf16)
    update = exchange(update.reshape((cols, -1) + update.shape[1:]), "col")
    rest_out = rest_rhs.astype(f32) - jnp.sum(update.astype(f32), axis=0)

    block_groups = [[k * width + i for i in range(width)] for k in range(BLOCKS)]
    base = exchange(repeat_for(forward.astype(f32) - trailing, width), "col", block_groups)
    base = jnp.transpose(base, (1, 0, 2)).reshape(both, NB)
    backward = jnp.zeros((both, tile_cols), bf16)
    reduced = jnp.zeros((both, NB), f32)
    carried = None
    for k in reversed(range(BLOCKS)):
        holder = col_block == k
        residual = (base - reduced).astype(bf16)
        value = solve(residual, upper_diagonal, half).astype(bf16)
        backward = jnp.where(holder, value, backward)
        if k > 0:
            solved = jnp.where(holder, value, jnp.zeros_like(value))
            order = [k - 1] + list(range(k - 1))
            reduced, carried = step(solved, carried, panel[: k * NB], order, k, k - 1)
            carried = jnp.where(col_block == k - 1, carried, 0.0)
    solution_rows = exchange(repeat_for(backward, rows), "row")
    solution_rows = jnp.transpose(solution_rows.reshape(rows, 2, half, tile_cols), (1, 3, 0, 2))
    return solution_rows.reshape(2, tile_cols, sources), rest_out.astype(bf16)


def solution(mesh):
    placed = (
        P(None, "row", None),
        P(None, "row", "col"),
        P(None, "row", "col"),
        P(None, "row", "col"),
        P(None, "row", "col"),
        P(None, "row", "col"),
        P(("row", "col"), None, None),
    )
    return jax.shard_map(
        per_device,
        mesh=mesh,
        in_specs=placed,
        out_specs=(P(None, "col", None), P(("row", "col"), None, None)),
        check_vma=False,
    )
```

```python
import jax
import jax.numpy as jnp
from jax import lax
from jax.sharding import PartitionSpec as P

N = 4096
NB = 1024
BLOCKS = N // NB
AXIS_Y, AXIS_X = 8, 4
X_GROUPS = [[y * AXIS_X + x for x in range(AXIS_X)] for y in range(AXIS_Y)]
Y_GROUPS = [[y * AXIS_X + x for y in range(AXIS_Y)] for x in range(AXIS_X)]


def nt(left, right):
    return lax.dot_general(left, right, (((1,), (1,)), ((), ())), preferred_element_type=jnp.float32)


def nn(left, right):
    return jnp.dot(left, right, preferred_element_type=jnp.float32)


def pair_groups(first, second, width):
    others = [k for k in range(BLOCKS) if k not in (first, second)]

    def members(k):
        return [k * width + i for i in range(width)]

    return [members(first) + members(second), members(others[0]) + members(others[1])]


def exchange(value, axis, groups=None):
    return lax.all_to_all(value, axis, 0, 0, axis_index_groups=groups)


def repeat_for(value, count):
    return jnp.broadcast_to(value[None], (count,) + value.shape)


def solve(residual, stored, half):
    width = stored.shape[1] // 2
    product = nn(residual, stored)
    real = product[:half, :width] - product[half:, width:]
    imag = product[:half, width:] + product[half:, :width]
    return jnp.concatenate([real, imag], axis=0)


def spread(solved, panel, half):
    real, imag = solved[:half], solved[half:]
    left = jnp.concatenate(
        [jnp.concatenate([real, -imag], axis=1), jnp.concatenate([imag, real], axis=1)], axis=0
    )
    return nt(left, panel)


def per_device(rhs, lower_factor, upper_factor, lower_rest, upper_rest, rest_solution, rest_rhs):
    rows, cols = lax.axis_size("row"), lax.axis_size("col")
    row_index = lax.axis_index("row")
    col_index = lax.axis_index("col")
    tile_rows = lower_factor.shape[1]
    tile_cols = lower_factor.shape[2]
    sources = rhs.shape[2]
    half = sources // rows
    both = 2 * half
    row_width = rows // BLOCKS
    width = cols // BLOCKS
    row_block = row_index // row_width
    col_block = col_index // width
    place = col_index % width
    bf16, f32 = jnp.bfloat16, jnp.float32

    tile = jnp.where(row_block >= col_block, lower_factor, upper_factor)
    tiles = jnp.stack([jnp.concatenate([t[0], t[1]], axis=1) for t in (tile, upper_factor)])
    near_tiles = exchange(repeat_for(tiles, AXIS_X), "row", X_GROUPS)
    panel = lax.all_gather(
        near_tiles[:, 0].reshape(-1, 2 * tile_cols), "row", axis=0, tiled=True, axis_index_groups=Y_GROUPS
    )

    by_source = jnp.transpose(rhs, (0, 2, 1)).reshape(2, rows, half, tile_rows)
    by_source = jnp.transpose(by_source, (1, 0, 2, 3))
    sent = jnp.concatenate([by_source, repeat_for(rest_solution, rows)], axis=3)
    sent, near_upper = lax.optimization_barrier((sent, near_tiles[:, 1]))
    got = exchange(sent, "row")
    got, near_upper = lax.optimization_barrier((got, near_upper))
    upper_panel = lax.all_gather(
        near_upper.reshape(-1, 2 * tile_cols), "row", axis=0, tiled=True, axis_index_groups=Y_GROUPS
    )
    own_rhs = lax.dynamic_slice_in_dim(got[..., :tile_rows], col_block * row_width, row_width, 0)
    own_rhs = jnp.transpose(own_rhs, (1, 2, 0, 3)).reshape(both, NB).astype(f32)

    rest = jnp.transpose(got[..., tile_rows:], (1, 0, 2, 3)).reshape(2, sources, -1)
    real = nt(rest[0], upper_rest[0]) - nt(rest[1], upper_rest[1])
    imag = nt(rest[0], upper_rest[1]) + nt(rest[1], upper_rest[0])
    trailing = jnp.stack([real, imag]).astype(bf16).reshape(2, rows, half, tile_rows)
    trailing = jnp.transpose(trailing, (1, 0, 2, 3))
    trailing, own_rhs = lax.optimization_barrier((trailing, own_rhs))
    trailing = exchange(trailing, "row")
    per_col = rows // cols
    trailing = exchange(trailing.reshape(cols, per_col, 2, half, tile_rows), "col")
    trailing = jnp.sum(trailing.astype(f32), axis=0)
    trailing = jnp.transpose(trailing, (1, 2, 0, 3)).reshape(both, tile_cols)
    panel, trailing, own_rhs = lax.optimization_barrier((panel, trailing, own_rhs))

    def step(solved, carried, part, order, this, following, held):
        count = len(order)
        products = spread(solved, part, half).reshape(both, count, width, tile_cols)
        if carried is not None:
            at_place = (lax.iota(jnp.int32, width) == place)[None, None, :, None]
            products = products + jnp.where(at_place, carried[:, :, None, :], 0.0)
        products = products.astype(bf16)
        near = repeat_for(products[:, order[0]].reshape(both, NB), width)
        pieces = [near]
        for later in order[1:]:
            pieces.append(jnp.transpose(products[:, later], (1, 0, 2)))
        payload = jnp.concatenate(pieces, axis=2)
        payload = jnp.concatenate([payload, payload], axis=0)
        payload, held = lax.optimization_barrier((payload, held))
        arrived = exchange(payload, "col", pair_groups(this, following, width))
        arrived = jnp.sum(arrived[:width].astype(f32), axis=0)
        return arrived[:, :NB], arrived[:, NB:].reshape(both, count - 1, tile_cols), held

    forward = jnp.zeros((both, tile_cols), bf16)
    reduced = jnp.zeros((both, NB), f32)
    carried = None
    for k in range(BLOCKS):
        holder = col_block == k
        residual = (own_rhs - reduced).astype(bf16)
        value = solve(residual, panel[k * NB : (k + 1) * NB], half).astype(bf16)
        forward = jnp.where(holder, value, forward)
        if k < BLOCKS - 1:
            solved = jnp.where(holder, value, jnp.zeros_like(value))
            count = BLOCKS - 1 - k
            reduced, carried, forward = step(
                solved, carried, panel[(k + 1) * NB :], list(range(count)), k, k + 1, forward
            )
            carried = jnp.where(col_block == k + 1, carried, 0.0)

    block_groups = [[k * width + i for i in range(width)] for k in range(BLOCKS)]
    base = exchange(repeat_for(forward.astype(f32) - trailing, width), "col", block_groups)
    base = jnp.transpose(base, (1, 0, 2)).reshape(both, NB)
    upper_diagonal = lax.dynamic_slice_in_dim(upper_panel, col_block * NB, NB, 0)
    backward = jnp.zeros((both, tile_cols), bf16)
    reduced = jnp.zeros((both, NB), f32)
    carried = None
    for k in reversed(range(BLOCKS)):
        holder = col_block == k
        residual = (base - reduced).astype(bf16)
        value = solve(residual, upper_diagonal, half).astype(bf16)
        backward = jnp.where(holder, value, backward)
        if k > 0:
            solved = jnp.where(holder, value, jnp.zeros_like(value))
            order = [k - 1] + list(range(k - 1))
            reduced, carried, backward = step(
                solved, carried, panel[: k * NB], order, k, k - 1, backward
            )
            carried = jnp.where(col_block == k - 1, carried, 0.0)

    solved_all = exchange(repeat_for(jnp.concatenate([forward, backward], axis=1), rows), "row")
    solved_all = solved_all.reshape(rows, 2, half, 2 * tile_cols)
    forward_all = jnp.transpose(solved_all[..., :tile_cols], (1, 0, 2, 3)).reshape(2, sources, tile_cols)
    solution_rows = jnp.transpose(solved_all[..., tile_cols:], (1, 3, 0, 2))

    real = nt(lower_rest[0], forward_all[0]) - nt(lower_rest[1], forward_all[1])
    imag = nt(lower_rest[0], forward_all[1]) + nt(lower_rest[1], forward_all[0])
    update = jnp.stack([real, imag], axis=1).astype(bf16)
    update = exchange(update.reshape((cols, -1) + update.shape[1:]), "col")
    rest_out = rest_rhs.astype(f32) - jnp.sum(update.astype(f32), axis=0)
    return solution_rows.reshape(2, tile_cols, sources), rest_out.astype(bf16)


def solution(mesh):
    placed = (
        P(None, "row", None),
        P(None, "row", "col"),
        P(None, "row", "col"),
        P(None, "row", "col"),
        P(None, "row", "col"),
        P(None, "row", "col"),
        P(("row", "col"), None, None),
    )
    return jax.shard_map(
        per_device,
        mesh=mesh,
        in_specs=placed,
        out_specs=(P(None, "col", None), P(("row", "col"), None, None)),
        check_vma=False,
    )
```

```python
import jax
import jax.numpy as jnp
from jax import lax
from jax.sharding import PartitionSpec as P

N = 4096
NB = 1024
BLOCKS = N // NB
AXIS_Y, AXIS_X = 8, 4
X_GROUPS = [[y * AXIS_X + x for x in range(AXIS_X)] for y in range(AXIS_Y)]
Y_GROUPS = [[y * AXIS_X + x for y in range(AXIS_Y)] for x in range(AXIS_X)]


def nt(left, right):
    return lax.dot_general(left, right, (((1,), (1,)), ((), ())), preferred_element_type=jnp.float32)


def nn(left, right):
    return jnp.dot(left, right, preferred_element_type=jnp.float32)


def pair_groups(first, second, width):
    def members(k):
        return [k * width + i for i in range(width)]

    return [members(first[0]) + members(first[1]), members(second[0]) + members(second[1])]


def exchange(value, axis, groups=None):
    return lax.all_to_all(value, axis, 0, 0, axis_index_groups=groups)


def repeat_for(value, count):
    return jnp.broadcast_to(value[None], (count,) + value.shape)


def solve(residual, stored, half):
    width = stored.shape[1] // 2
    product = nn(residual, stored)
    real = product[:half, :width] - product[half:, width:]
    imag = product[:half, width:] + product[half:, :width]
    return jnp.concatenate([real, imag], axis=0)


def spread(solved, panel, half):
    real, imag = solved[:half], solved[half:]
    left = jnp.concatenate(
        [jnp.concatenate([real, -imag], axis=1), jnp.concatenate([imag, real], axis=1)], axis=0
    )
    return nt(left, panel)


def per_device(rhs, lower_factor, upper_factor, lower_rest, upper_rest, rest_solution, rest_rhs):
    rows, cols = lax.axis_size("row"), lax.axis_size("col")
    row_index = lax.axis_index("row")
    col_index = lax.axis_index("col")
    tile_rows = lower_factor.shape[1]
    tile_cols = lower_factor.shape[2]
    sources = rhs.shape[2]
    half = sources // rows
    both = 2 * half
    row_width = rows // BLOCKS
    width = cols // BLOCKS
    row_block = row_index // row_width
    col_block = col_index // width
    place = col_index % width
    bf16, f32 = jnp.bfloat16, jnp.float32

    tile = jnp.where(row_block >= col_block, lower_factor, upper_factor)
    tiles = jnp.stack([jnp.concatenate([t[0], t[1]], axis=1) for t in (tile, upper_factor)])
    near_tiles = exchange(repeat_for(tiles, AXIS_X), "row", X_GROUPS)
    panel = lax.all_gather(
        near_tiles[:, 0].reshape(-1, 2 * tile_cols), "row", axis=0, tiled=True, axis_index_groups=Y_GROUPS
    )

    by_source = jnp.transpose(rhs, (0, 2, 1)).reshape(2, rows, half, tile_rows)
    by_source = jnp.transpose(by_source, (1, 0, 2, 3))
    sent = jnp.concatenate([by_source, repeat_for(rest_solution, rows)], axis=3)
    sent, near_upper = lax.optimization_barrier((sent, near_tiles[:, 1]))
    got = exchange(sent, "row")
    got, near_upper = lax.optimization_barrier((got, near_upper))
    upper_panel = lax.all_gather(
        near_upper.reshape(-1, 2 * tile_cols), "row", axis=0, tiled=True, axis_index_groups=Y_GROUPS
    )
    own_rhs = lax.dynamic_slice_in_dim(got[..., :tile_rows], col_block * row_width, row_width, 0)
    own_rhs = jnp.transpose(own_rhs, (1, 2, 0, 3)).reshape(both, NB).astype(f32)

    rest = jnp.transpose(got[..., tile_rows:], (1, 0, 2, 3)).reshape(2, sources, -1)
    real = nt(rest[0], upper_rest[0]) - nt(rest[1], upper_rest[1])
    imag = nt(rest[0], upper_rest[1]) + nt(rest[1], upper_rest[0])
    trailing = jnp.stack([real, imag]).astype(bf16).reshape(2, rows, half, tile_rows)
    trailing = jnp.transpose(trailing, (1, 0, 2, 3))
    trailing, own_rhs = lax.optimization_barrier((trailing, own_rhs))
    trailing = exchange(trailing, "row")
    per_col = rows // cols
    trailing = exchange(trailing.reshape(cols, per_col, 2, half, tile_rows), "col")
    trailing = jnp.sum(trailing.astype(f32), axis=0)
    trailing = jnp.transpose(trailing, (1, 2, 0, 3)).reshape(both, tile_cols)
    panel, trailing, own_rhs = lax.optimization_barrier((panel, trailing, own_rhs))

    at_place = (lax.iota(jnp.int32, width) == place)[None, :, None]

    def chain(sequence, start, diagonal, kept):
        reduced = jnp.zeros((both, NB), f32)
        carried = None
        for stage, k in enumerate(sequence):
            holder = col_block == k
            residual = (start - reduced).astype(bf16)
            value = solve(residual, diagonal(k), half).astype(bf16)
            kept = jnp.where(holder, value, kept)
            later = sequence[stage + 1 :]
            if not later:
                return kept
            solved = jnp.where(holder, value, jnp.zeros_like(value))
            low, high = min(later), max(later) + 1
            products = spread(solved, panel[low * NB : high * NB], half)
            products = products.reshape(both, high - low, width, tile_cols)
            near = products[:, later[0] - low]
            if carried is not None:
                near = near + jnp.where(at_place, carried[:, None, :], 0.0)
            near = near.astype(bf16).reshape(both, NB)
            pieces = [repeat_for(near, width)]
            if stage == 0:
                last = products[:, later[2] - low].astype(bf16).reshape(both, NB)
            if stage == 1:
                pieces = [repeat_for(jnp.where(col_block == sequence[0], last, near), width)]
            if len(later) > 1:
                pieces.append(jnp.transpose(products[:, later[1] - low].astype(bf16), (1, 0, 2)))
            payload = jnp.concatenate(pieces, axis=2)
            payload = jnp.concatenate([payload, payload], axis=0)
            payload, kept = lax.optimization_barrier((payload, kept))
            others = [j for j in sequence if j not in (k, later[0])]
            arrived = exchange(payload, "col", pair_groups((k, later[0]), others, width))
            arrived = jnp.sum(arrived[:width].astype(f32), axis=0)
            reduced = reduced + arrived[:, :NB]
            if len(later) > 1:
                carried = jnp.where(col_block == later[0], arrived[:, NB:], 0.0)

    empty = jnp.zeros((both, tile_cols), bf16)
    forward = chain([0, 1, 2, 3], own_rhs, lambda k: panel[k * NB : (k + 1) * NB], empty)

    block_groups = [[k * width + i for i in range(width)] for k in range(BLOCKS)]
    base = exchange(repeat_for((forward.astype(f32) - trailing).astype(bf16), width), "col", block_groups)
    base = jnp.transpose(base, (1, 0, 2)).reshape(both, NB).astype(f32)
    upper_diagonal = lax.dynamic_slice_in_dim(upper_panel, col_block * NB, NB, 0)
    backward = chain([3, 2, 1, 0], base, lambda k: upper_diagonal, empty)

    solved_all = exchange(repeat_for(jnp.concatenate([forward, backward], axis=1), AXIS_Y), "row", Y_GROUPS)
    solved_all = exchange(repeat_for(solved_all, AXIS_X), "row", X_GROUPS)
    solved_all = solved_all.reshape(AXIS_X, AXIS_Y, 2, half, 2 * tile_cols)
    forward_all = jnp.transpose(solved_all[..., :tile_cols], (2, 1, 0, 3, 4)).reshape(2, sources, tile_cols)
    solution_rows = jnp.transpose(solved_all[..., tile_cols:], (2, 4, 1, 0, 3))

    real = nt(lower_rest[0], forward_all[0]) - nt(lower_rest[1], forward_all[1])
    imag = nt(lower_rest[0], forward_all[1]) + nt(lower_rest[1], forward_all[0])
    update = jnp.stack([real, imag], axis=1).astype(bf16)
    update = exchange(update.reshape((cols, -1) + update.shape[1:]), "col")
    rest_out = rest_rhs.astype(f32) - jnp.sum(update.astype(f32), axis=0)
    return solution_rows.reshape(2, tile_cols, sources), rest_out.astype(bf16)


def solution(mesh):
    placed = (
        P(None, "row", None),
        P(None, "row", "col"),
        P(None, "row", "col"),
        P(None, "row", "col"),
        P(None, "row", "col"),
        P(None, "row", "col"),
        P(("row", "col"), None, None),
    )
    return jax.shard_map(
        per_device,
        mesh=mesh,
        in_specs=placed,
        out_specs=(P(None, "col", None), P(("row", "col"), None, None)),
        check_vma=False,
    )
```

```python
import jax
import jax.numpy as jnp
from jax import lax
from jax.sharding import PartitionSpec as P

N = 4096
NB = 1024
BLOCKS = N // NB
AXIS_Y, AXIS_X = 8, 4
X_GROUPS = [[y * AXIS_X + x for x in range(AXIS_X)] for y in range(AXIS_Y)]
Y_GROUPS = [[y * AXIS_X + x for y in range(AXIS_Y)] for x in range(AXIS_X)]


def nt(left, right):
    return lax.dot_general(left, right, (((1,), (1,)), ((), ())), preferred_element_type=jnp.float32)


def nn(left, right):
    return jnp.dot(left, right, preferred_element_type=jnp.float32)


def pair_groups(first, second, width):
    def members(k):
        return [k * width + i for i in range(width)]

    return [members(first[0]) + members(first[1]), members(second[0]) + members(second[1])]


def exchange(value, axis, groups=None):
    return lax.all_to_all(value, axis, 0, 0, axis_index_groups=groups)


def repeat_for(value, count):
    return jnp.broadcast_to(value[None], (count,) + value.shape)


def solve(residual, stored, half):
    width = stored.shape[1] // 2
    product = nn(residual, stored)
    real = product[:half, :width] - product[half:, width:]
    imag = product[:half, width:] + product[half:, :width]
    return jnp.concatenate([real, imag], axis=0)


def spread(solved, panel, half):
    real, imag = solved[:half], solved[half:]
    left = jnp.concatenate(
        [jnp.concatenate([real, -imag], axis=1), jnp.concatenate([imag, real], axis=1)], axis=0
    )
    return nt(left, panel)


def per_device(rhs, lower_factor, upper_factor, lower_rest, upper_rest, rest_solution, rest_rhs):
    rows, cols = lax.axis_size("row"), lax.axis_size("col")
    row_index = lax.axis_index("row")
    col_index = lax.axis_index("col")
    tile_rows = lower_factor.shape[1]
    tile_cols = lower_factor.shape[2]
    sources = rhs.shape[2]
    half = sources // rows
    both = 2 * half
    row_width = rows // BLOCKS
    width = cols // BLOCKS
    row_block = row_index // row_width
    col_block = col_index // width
    place = col_index % width
    bf16, f32 = jnp.bfloat16, jnp.float32

    tile = jnp.where(row_block >= col_block, lower_factor, upper_factor)
    tiles = jnp.concatenate([jnp.concatenate([t[0], t[1]], axis=1) for t in (tile, upper_factor)], axis=0)
    lanes = 2 * tile_cols // tile_rows
    by_source = jnp.transpose(rhs, (0, 2, 1))
    by_source = by_source.reshape(2, lanes, AXIS_Y // lanes, AXIS_X, half, tile_rows)
    by_source = jnp.transpose(by_source, (3, 0, 2, 4, 1, 5)).reshape(AXIS_X, -1, 2 * tile_cols)
    near = exchange(jnp.concatenate([repeat_for(tiles, AXIS_X), by_source], axis=1), "row", X_GROUPS)

    panel = lax.all_gather(
        near[:, :tile_rows].reshape(-1, 2 * tile_cols), "row", axis=0, tiled=True, axis_index_groups=Y_GROUPS
    )
    near_upper = near[:, tile_rows : 2 * tile_rows].reshape(-1, 2 * tile_cols)
    near_rhs = near[:, 2 * tile_rows :].reshape(AXIS_X, 2, AXIS_Y // lanes, half, lanes, tile_rows)
    near_rhs = jnp.transpose(near_rhs, (4, 2, 1, 3, 0, 5)).reshape(AXIS_Y, both, AXIS_X * tile_rows)
    near_rest = repeat_for(rest_solution.reshape(both, -1), AXIS_Y)
    sent = jnp.concatenate([near_rhs, near_rest], axis=2)
    sent, near_upper, upper_rest = lax.optimization_barrier((sent, near_upper, upper_rest))
    got = exchange(sent, "row", Y_GROUPS)
    got, near_upper, upper_rest = lax.optimization_barrier((got, near_upper, upper_rest))
    upper_panel = lax.all_gather(near_upper, "row", axis=0, tiled=True, axis_index_groups=Y_GROUPS)
    wide_rows = AXIS_X * tile_rows
    per_block = AXIS_Y // BLOCKS
    own_rhs = lax.dynamic_slice_in_dim(got[..., :wide_rows], col_block * per_block, per_block, 0)
    own_rhs = jnp.transpose(own_rhs, (1, 0, 2)).reshape(both, NB).astype(f32)

    rest = got[..., wide_rows:].reshape(AXIS_Y, 2, half, -1)
    rest = jnp.transpose(rest, (1, 0, 2, 3)).reshape(2, AXIS_Y * half, -1)
    wide = exchange(repeat_for(upper_rest, AXIS_X), "row", X_GROUPS)
    wide = jnp.transpose(wide, (1, 0, 2, 3)).reshape(2, wide_rows, -1)
    real = nt(rest[0], wide[0]) - nt(rest[1], wide[1])
    imag = nt(rest[0], wide[1]) + nt(rest[1], wide[0])
    trailing = jnp.stack([real, imag]).astype(bf16).reshape(2, AXIS_Y, half, wide_rows)
    trailing = jnp.transpose(trailing, (1, 0, 2, 3)).reshape(AXIS_Y, both, wide_rows)
    trailing, own_rhs = lax.optimization_barrier((trailing, own_rhs))
    trailing = exchange(trailing, "row", Y_GROUPS)
    trailing = trailing.reshape(AXIS_Y, both, cols // AXIS_Y, tile_cols)
    trailing = jnp.transpose(trailing, (0, 2, 1, 3)).reshape(cols, both, tile_cols)
    trailing = jnp.sum(exchange(trailing, "col").astype(f32), axis=0)
    panel, trailing, own_rhs = lax.optimization_barrier((panel, trailing, own_rhs))

    at_place = (lax.iota(jnp.int32, width) == place)[None, :, None]

    def chain(sequence, start, diagonal, kept):
        reduced = jnp.zeros((both, NB), f32)
        carried = None
        for stage, k in enumerate(sequence):
            holder = col_block == k
            residual = (start - reduced).astype(bf16)
            value = solve(residual, diagonal(k), half).astype(bf16)
            kept = jnp.where(holder, value, kept)
            later = sequence[stage + 1 :]
            if not later:
                return kept
            solved = jnp.where(holder, value, jnp.zeros_like(value))
            low, high = min(later), max(later) + 1
            products = spread(solved, panel[low * NB : high * NB], half)
            products = products.reshape(both, high - low, width, tile_cols)
            near = products[:, later[0] - low]
            if carried is not None:
                near = near + jnp.where(at_place, carried[:, None, :], 0.0)
            near = near.astype(bf16).reshape(both, NB)
            pieces = [repeat_for(near, width)]
            if stage == 0:
                last = products[:, later[2] - low].astype(bf16).reshape(both, NB)
            if stage == 1:
                pieces = [repeat_for(jnp.where(col_block == sequence[0], last, near), width)]
            if len(later) > 1:
                pieces.append(jnp.transpose(products[:, later[1] - low].astype(bf16), (1, 0, 2)))
            payload = jnp.concatenate(pieces, axis=2)
            payload = jnp.concatenate([payload, payload], axis=0)
            payload, kept = lax.optimization_barrier((payload, kept))
            others = [j for j in sequence if j not in (k, later[0])]
            arrived = exchange(payload, "col", pair_groups((k, later[0]), others, width))
            arrived = jnp.sum(arrived[:width].astype(f32), axis=0)
            reduced = reduced + arrived[:, :NB]
            if len(later) > 1:
                carried = jnp.where(col_block == later[0], arrived[:, NB:], 0.0)

    empty = jnp.zeros((both, tile_cols), bf16)
    forward = chain([0, 1, 2, 3], own_rhs, lambda k: panel[k * NB : (k + 1) * NB], empty)

    block_groups = [[k * width + i for i in range(width)] for k in range(BLOCKS)]
    base = exchange(repeat_for((forward.astype(f32) - trailing).astype(bf16), width), "col", block_groups)
    base = jnp.transpose(base, (1, 0, 2)).reshape(both, NB).astype(f32)
    upper_diagonal = lax.dynamic_slice_in_dim(upper_panel, col_block * NB, NB, 0)
    backward = chain([3, 2, 1, 0], base, lambda k: upper_diagonal, empty)

    solved_all = exchange(repeat_for(jnp.concatenate([forward, backward], axis=1), rows), "row")
    solved_all = solved_all.reshape(rows, 2, half, 2 * tile_cols)
    forward_all = jnp.transpose(solved_all[..., :tile_cols], (1, 0, 2, 3)).reshape(2, sources, tile_cols)
    solution_rows = jnp.transpose(solved_all[..., tile_cols:], (1, 3, 0, 2))

    real = nt(lower_rest[0], forward_all[0]) - nt(lower_rest[1], forward_all[1])
    imag = nt(lower_rest[0], forward_all[1]) + nt(lower_rest[1], forward_all[0])
    update = jnp.stack([real, imag], axis=1).astype(bf16)
    update = exchange(update.reshape((cols, -1) + update.shape[1:]), "col")
    rest_out = rest_rhs.astype(f32) - jnp.sum(update.astype(f32), axis=0)
    return solution_rows.reshape(2, tile_cols, sources), rest_out.astype(bf16)


def solution(mesh):
    placed = (
        P(None, "row", None),
        P(None, "row", "col"),
        P(None, "row", "col"),
        P(None, "row", "col"),
        P(None, "row", "col"),
        P(None, "row", "col"),
        P(("row", "col"), None, None),
    )
    return jax.shard_map(
        per_device,
        mesh=mesh,
        in_specs=placed,
        out_specs=(P(None, "col", None), P(("row", "col"), None, None)),
        check_vma=False,
    )
```

```python
import functools

import jax
import jax.numpy as jnp
from jax import lax
from jax.experimental import pallas as pl
from jax.experimental.pallas import tpu as pltpu
from jax.sharding import PartitionSpec as P

N = 4096
NB = 1024
BLOCKS = N // NB
AXIS_Y, AXIS_X = 8, 4
X_GROUPS = [[y * AXIS_X + x for x in range(AXIS_X)] for y in range(AXIS_Y)]
Y_GROUPS = [[y * AXIS_X + x for y in range(AXIS_Y)] for x in range(AXIS_X)]


def nt(left, right):
    return lax.dot_general(left, right, (((1,), (1,)), ((), ())), preferred_element_type=jnp.float32)


def nn(left, right):
    return jnp.dot(left, right, preferred_element_type=jnp.float32)


def pair_groups(first, second, width):
    def members(k):
        return [k * width + i for i in range(width)]

    return [members(first[0]) + members(first[1]), members(second[0]) + members(second[1])]


def exchange(value, axis, groups=None):
    return lax.all_to_all(value, axis, 0, 0, axis_index_groups=groups)


def repeat_for(value, count):
    return jnp.broadcast_to(value[None], (count,) + value.shape)


def stage_kernel(sequence, stage, width, moving, *refs):
    k, later = sequence[stage], sequence[stage + 1 :]
    refs = list(refs)
    where, start, kept = refs[:3]
    rest = refs[3:]
    arrived = rest.pop(0) if stage else None
    before = rest.pop(0) if stage == 3 else None
    last_in = rest.pop(0) if stage == 1 else None
    diagonal = rest.pop(0)
    panel = rest.pop(0) if later else None
    kept_out = rest.pop(0)
    payload = rest.pop(0) if later else None
    reduced_out = rest.pop(0) if stage == 2 else None
    last_out = rest.pop(0) if stage == 0 else None
    diagonal_buf, diagonal_sem = rest.pop(0), rest.pop(0)
    bf16, f32 = jnp.bfloat16, jnp.float32
    block, place = where[0], where[1]

    first = pl.multiple_of(block * NB, NB) if moving else k * NB
    copy = pltpu.make_async_copy(diagonal.at[pl.ds(first, NB)], diagonal_buf, diagonal_sem)
    copy.start()
    panel_copies = []
    if later:
        panel_buf, panel_sem = rest.pop(0), rest.pop(0)
        for i, j in enumerate(later):
            panel_copies.append(
                pltpu.make_async_copy(panel.at[pl.ds(j * NB, NB)], panel_buf.at[i], panel_sem.at[i])
            )
            panel_copies[i].start()

    both = start.shape[0]
    half = both // 2
    tile_cols = kept.shape[1]
    residual = start[...]
    arrival = None
    if stage:
        arrival = arrived[0].astype(f32)
        for i in range(1, width):
            arrival = arrival + arrived[i].astype(f32)
        reduced = arrival[:, :NB]
        if stage == 3:
            reduced = reduced + before[...]
        if stage == 2:
            reduced_out[...] = reduced
        residual = residual - reduced
    residual = residual.astype(bf16)
    holder = block == k
    copy.wait()
    product = nn(residual, diagonal_buf[...])
    real = product[:half, :tile_cols] - product[half:, tile_cols:]
    imag = product[:half, tile_cols:] + product[half:, :tile_cols]
    value = jnp.concatenate([real, imag], axis=0).astype(bf16)
    kept_out[...] = jnp.where(holder, value, kept[...])
    if not later:
        return
    solved = jnp.where(holder, value, jnp.zeros_like(value)).astype(f32)
    real, imag = solved[:half], solved[half:]
    left = jnp.concatenate(
        [jnp.concatenate([real, -imag], axis=1), jnp.concatenate([imag, real], axis=1)], axis=0
    ).astype(bf16)
    panel_copies[0].wait()
    near = nt(left, panel_buf[0])
    carried = None
    if stage and arrival.shape[1] > NB:
        carried = arrival[:, NB:]
    for q in range(width):
        columns = slice(q * tile_cols, (q + 1) * tile_cols)
        piece = near[:, columns]
        if carried is not None:
            piece = piece + jnp.where(holder & (place == q), carried, 0.0)
        piece = piece.astype(bf16)
        if stage == 1:
            piece = jnp.where(block == sequence[0], last_in[:, columns], piece)
        for target in range(2 * width):
            payload[target, :, columns] = piece
    if len(later) > 1:
        panel_copies[1].wait()
        far = nt(left, panel_buf[1]).astype(bf16)
        for target in range(2 * width):
            q = target % width
            payload[target, :, NB:] = far[:, q * tile_cols : (q + 1) * tile_cols]
    if stage == 0:
        panel_copies[2].wait()
        last_out[...] = nt(left, panel_buf[2]).astype(bf16)


def run_stage(sequence, stage, width, moving, where, start, kept, extra, diagonal, panel):
    later = len(sequence) - 1 - stage
    both, tile_cols = kept.shape
    bf16, f32 = jnp.bfloat16, jnp.float32
    operands = [where, start, kept, *extra, diagonal]
    vmem, anywhere = pl.BlockSpec(memory_space=pltpu.VMEM), pl.BlockSpec(memory_space=pl.ANY)
    in_specs = [pl.BlockSpec(memory_space=pltpu.SMEM)] + [vmem] * (2 + len(extra)) + [anywhere]
    out_shape = [jax.ShapeDtypeStruct(kept.shape, bf16)]
    scratch = [pltpu.VMEM((NB, 2 * tile_cols), bf16), pltpu.SemaphoreType.DMA]
    if later:
        operands.append(panel)
        in_specs.append(anywhere)
        wide = NB + (tile_cols if later > 1 else 0)
        out_shape.append(jax.ShapeDtypeStruct((2 * width, both, wide), bf16))
        scratch += [pltpu.VMEM((later, NB, 2 * tile_cols), bf16), pltpu.SemaphoreType.DMA((later,))]
    if stage == 2:
        out_shape.append(jax.ShapeDtypeStruct((both, NB), f32))
    if stage == 0:
        out_shape.append(jax.ShapeDtypeStruct((both, NB), bf16))
    return pl.pallas_call(
        functools.partial(stage_kernel, sequence, stage, width, moving),
        out_shape=out_shape,
        in_specs=in_specs,
        out_specs=[vmem] * len(out_shape),
        scratch_shapes=scratch,
        compiler_params=pltpu.CompilerParams(vmem_limit_bytes=14 * 2**20),
        cost_estimate=pl.CostEstimate(
            flops=4 * both * NB * tile_cols * (1 + later),
            bytes_accessed=4 * NB * tile_cols * (1 + later),
            transcendentals=0,
        ),
        name=f"stage{stage}",
    )(*operands)


def per_device(rhs, lower_factor, upper_factor, lower_rest, upper_rest, rest_solution, rest_rhs):
    rows, cols = lax.axis_size("row"), lax.axis_size("col")
    row_index = lax.axis_index("row")
    col_index = lax.axis_index("col")
    tile_rows = lower_factor.shape[1]
    tile_cols = lower_factor.shape[2]
    sources = rhs.shape[2]
    half = sources // rows
    both = 2 * half
    row_width = rows // BLOCKS
    width = cols // BLOCKS
    row_block = row_index // row_width
    col_block = col_index // width
    place = col_index % width
    bf16, f32 = jnp.bfloat16, jnp.float32

    tile = jnp.where(row_block >= col_block, lower_factor, upper_factor)
    tiles = jnp.concatenate([jnp.concatenate([t[0], t[1]], axis=1) for t in (tile, upper_factor)], axis=0)
    lanes = 2 * tile_cols // tile_rows
    by_source = jnp.transpose(rhs, (0, 2, 1))
    by_source = by_source.reshape(2, lanes, AXIS_Y // lanes, AXIS_X, half, tile_rows)
    by_source = jnp.transpose(by_source, (3, 0, 2, 4, 1, 5)).reshape(AXIS_X, -1, 2 * tile_cols)
    near = exchange(jnp.concatenate([repeat_for(tiles, AXIS_X), by_source], axis=1), "row", X_GROUPS)

    panel = lax.all_gather(
        near[:, :tile_rows].reshape(-1, 2 * tile_cols), "row", axis=0, tiled=True, axis_index_groups=Y_GROUPS
    )
    near_upper = near[:, tile_rows : 2 * tile_rows].reshape(-1, 2 * tile_cols)
    near_rhs = near[:, 2 * tile_rows :].reshape(AXIS_X, 2, AXIS_Y // lanes, half, lanes, tile_rows)
    near_rhs = jnp.transpose(near_rhs, (4, 2, 1, 3, 0, 5)).reshape(AXIS_Y, both, AXIS_X * tile_rows)
    near_rest = repeat_for(rest_solution.reshape(both, -1), AXIS_Y)
    sent = jnp.concatenate([near_rhs, near_rest], axis=2)
    sent, near_upper, upper_rest = lax.optimization_barrier((sent, near_upper, upper_rest))
    got = exchange(sent, "row", Y_GROUPS)
    got, near_upper, upper_rest = lax.optimization_barrier((got, near_upper, upper_rest))
    upper_panel = lax.all_gather(near_upper, "row", axis=0, tiled=True, axis_index_groups=Y_GROUPS)
    wide_rows = AXIS_X * tile_rows
    per_block = AXIS_Y // BLOCKS
    own_rhs = lax.dynamic_slice_in_dim(got[..., :wide_rows], col_block * per_block, per_block, 0)
    own_rhs = jnp.transpose(own_rhs, (1, 0, 2)).reshape(both, NB).astype(f32)

    rest = got[..., wide_rows:].reshape(AXIS_Y, 2, half, -1)
    rest = jnp.transpose(rest, (1, 0, 2, 3)).reshape(2, AXIS_Y * half, -1)
    wide = exchange(repeat_for(upper_rest, AXIS_X), "row", X_GROUPS)
    wide = jnp.transpose(wide, (1, 0, 2, 3)).reshape(2, wide_rows, -1)
    real = nt(rest[0], wide[0]) - nt(rest[1], wide[1])
    imag = nt(rest[0], wide[1]) + nt(rest[1], wide[0])
    trailing = jnp.stack([real, imag]).astype(bf16).reshape(2, AXIS_Y, half, wide_rows)
    trailing = jnp.transpose(trailing, (1, 0, 2, 3)).reshape(AXIS_Y, both, wide_rows)
    trailing, own_rhs = lax.optimization_barrier((trailing, own_rhs))
    trailing = exchange(trailing, "row", Y_GROUPS)
    trailing = trailing.reshape(AXIS_Y, both, cols // AXIS_Y, tile_cols)
    trailing = jnp.transpose(trailing, (0, 2, 1, 3)).reshape(cols, both, tile_cols)
    trailing = jnp.sum(exchange(trailing, "col").astype(f32), axis=0)
    panel, trailing, own_rhs = lax.optimization_barrier((panel, trailing, own_rhs))

    where = jnp.stack([col_block, place]).astype(jnp.int32)

    def chain(sequence, start, diagonal, moving, kept):
        extra = []
        for stage, k in enumerate(sequence):
            outs = run_stage(sequence, stage, width, moving, where, start, kept, extra, diagonal, panel)
            kept = outs[0]
            if stage == len(sequence) - 1:
                return kept
            following = sequence[stage + 1]
            others = [j for j in sequence if j not in (k, following)]
            arrived = exchange(outs[1], "col", pair_groups((k, following), others, width))
            extra = [arrived, *outs[2:]]

    empty = jnp.zeros((both, tile_cols), bf16)
    forward = chain((0, 1, 2, 3), own_rhs, panel, False, empty)

    block_groups = [[k * width + i for i in range(width)] for k in range(BLOCKS)]
    base = exchange(repeat_for((forward.astype(f32) - trailing).astype(bf16), width), "col", block_groups)
    base = jnp.transpose(base, (1, 0, 2)).reshape(both, NB).astype(f32)
    backward = chain((3, 2, 1, 0), base, upper_panel, True, empty)

    solved_all = exchange(repeat_for(jnp.concatenate([forward, backward], axis=1), rows), "row")
    solved_all = solved_all.reshape(rows, 2, half, 2 * tile_cols)
    forward_all = jnp.transpose(solved_all[..., :tile_cols], (1, 0, 2, 3)).reshape(2, sources, tile_cols)
    solution_rows = jnp.transpose(solved_all[..., tile_cols:], (1, 3, 0, 2))

    real = nt(lower_rest[0], forward_all[0]) - nt(lower_rest[1], forward_all[1])
    imag = nt(lower_rest[0], forward_all[1]) + nt(lower_rest[1], forward_all[0])
    update = jnp.stack([real, imag], axis=1).astype(bf16)
    update = exchange(update.reshape((cols, -1) + update.shape[1:]), "col")
    rest_out = rest_rhs.astype(f32) - jnp.sum(update.astype(f32), axis=0)
    return solution_rows.reshape(2, tile_cols, sources), rest_out.astype(bf16)


def solution(mesh):
    placed = (
        P(None, "row", None),
        P(None, "row", "col"),
        P(None, "row", "col"),
        P(None, "row", "col"),
        P(None, "row", "col"),
        P(None, "row", "col"),
        P(("row", "col"), None, None),
    )
    return jax.shard_map(
        per_device,
        mesh=mesh,
        in_specs=placed,
        out_specs=(P(None, "col", None), P(("row", "col"), None, None)),
        check_vma=False,
    )
```

```python
import functools

import jax
import jax.numpy as jnp
from jax import lax
from jax.experimental import pallas as pl
from jax.experimental.pallas import tpu as pltpu
from jax.sharding import PartitionSpec as P

N = 4096
NB = 1024
BLOCKS = N // NB
AXIS_Y, AXIS_X = 8, 4
X_GROUPS = [[y * AXIS_X + x for x in range(AXIS_X)] for y in range(AXIS_Y)]
Y_GROUPS = [[y * AXIS_X + x for y in range(AXIS_Y)] for x in range(AXIS_X)]


def nt(left, right):
    return lax.dot_general(left, right, (((1,), (1,)), ((), ())), preferred_element_type=jnp.float32)


def nn(left, right):
    return jnp.dot(left, right, preferred_element_type=jnp.float32)


def pair_groups(first, second, width):
    def members(k):
        return [k * width + i for i in range(width)]

    return [members(first[0]) + members(first[1]), members(second[0]) + members(second[1])]


def exchange(value, axis, groups=None):
    return lax.all_to_all(value, axis, 0, 0, axis_index_groups=groups)


def repeat_for(value, count):
    return jnp.broadcast_to(value[None], (count,) + value.shape)


def stage_kernel(sequence, stage, width, *refs):
    k, later = sequence[stage], sequence[stage + 1 :]
    refs = list(refs)
    where, start, kept = refs[:3]
    rest = refs[3:]
    arrived = rest.pop(0) if stage else None
    before = rest.pop(0) if stage == 3 else None
    last_in = rest.pop(0) if stage == 1 else None
    diagonal = rest.pop(0)
    panel = rest.pop(0) if later else None
    kept_out = rest.pop(0)
    payload = rest.pop(0) if later else None
    reduced_out = rest.pop(0) if stage == 2 else None
    last_out = rest.pop(0) if stage == 0 else None
    diagonal_buf, diagonal_sem = rest.pop(0), rest.pop(0)
    bf16, f32 = jnp.bfloat16, jnp.float32
    block, place = where[0], where[1]

    first = 0 if diagonal.shape[0] == NB else k * NB
    copy = pltpu.make_async_copy(diagonal.at[pl.ds(first, NB)], diagonal_buf, diagonal_sem)
    copy.start()
    panel_copies = []
    if later:
        panel_buf, panel_sem = rest.pop(0), rest.pop(0)
        for i, j in enumerate(later):
            panel_copies.append(
                pltpu.make_async_copy(panel.at[pl.ds(j * NB, NB)], panel_buf.at[i], panel_sem.at[i])
            )
            panel_copies[i].start()

    both = start.shape[0]
    half = both // 2
    tile_cols = kept.shape[1]
    residual = start[...]
    arrival = None
    if stage:
        arrival = arrived[0].astype(f32)
        for i in range(1, width):
            arrival = arrival + arrived[i].astype(f32)
        reduced = arrival[:, :NB]
        if stage == 3:
            reduced = reduced + before[...]
        if stage == 2:
            reduced_out[...] = reduced
        residual = residual - reduced
    residual = residual.astype(bf16)
    holder = block == k
    copy.wait()
    product = nn(residual, diagonal_buf[...])
    real = product[:half, :tile_cols] - product[half:, tile_cols:]
    imag = product[:half, tile_cols:] + product[half:, :tile_cols]
    value = jnp.concatenate([real, imag], axis=0).astype(bf16)
    kept_out[...] = jnp.where(holder, value, kept[...])
    if not later:
        return
    solved = jnp.where(holder, value, jnp.zeros_like(value)).astype(f32)
    real, imag = solved[:half], solved[half:]
    left = jnp.concatenate(
        [jnp.concatenate([real, -imag], axis=1), jnp.concatenate([imag, real], axis=1)], axis=0
    ).astype(bf16)
    panel_copies[0].wait()
    near = nt(left, panel_buf[0])
    carried = None
    if stage and arrival.shape[1] > NB:
        carried = arrival[:, NB:]
    for q in range(width):
        columns = slice(q * tile_cols, (q + 1) * tile_cols)
        piece = near[:, columns]
        if carried is not None:
            piece = piece + jnp.where(holder & (place == q), carried, 0.0)
        piece = piece.astype(bf16)
        if stage == 1:
            piece = jnp.where(block == sequence[0], last_in[:, columns], piece)
        for target in range(2 * width):
            payload[target, :, columns] = piece
    if len(later) > 1:
        panel_copies[1].wait()
        far = nt(left, panel_buf[1]).astype(bf16)
        for target in range(2 * width):
            q = target % width
            payload[target, :, NB:] = far[:, q * tile_cols : (q + 1) * tile_cols]
    if stage == 0:
        panel_copies[2].wait()
        last_out[...] = nt(left, panel_buf[2]).astype(bf16)


def run_stage(sequence, stage, width, where, start, kept, extra, diagonal, panel):
    later = len(sequence) - 1 - stage
    both, tile_cols = kept.shape
    bf16, f32 = jnp.bfloat16, jnp.float32
    operands = [where, start, kept, *extra, diagonal]
    vmem, anywhere = pl.BlockSpec(memory_space=pltpu.VMEM), pl.BlockSpec(memory_space=pl.ANY)
    in_specs = [pl.BlockSpec(memory_space=pltpu.SMEM)] + [vmem] * (2 + len(extra)) + [anywhere]
    out_shape = [jax.ShapeDtypeStruct(kept.shape, bf16)]
    scratch = [pltpu.VMEM((NB, 2 * tile_cols), bf16), pltpu.SemaphoreType.DMA]
    if later:
        operands.append(panel)
        in_specs.append(anywhere)
        wide = NB + (tile_cols if later > 1 else 0)
        out_shape.append(jax.ShapeDtypeStruct((2 * width, both, wide), bf16))
        scratch += [pltpu.VMEM((later, NB, 2 * tile_cols), bf16), pltpu.SemaphoreType.DMA((later,))]
    if stage == 2:
        out_shape.append(jax.ShapeDtypeStruct((both, NB), f32))
    if stage == 0:
        out_shape.append(jax.ShapeDtypeStruct((both, NB), bf16))
    return pl.pallas_call(
        functools.partial(stage_kernel, sequence, stage, width),
        out_shape=out_shape,
        in_specs=in_specs,
        out_specs=[vmem] * len(out_shape),
        scratch_shapes=scratch,
        compiler_params=pltpu.CompilerParams(vmem_limit_bytes=14 * 2**20),
        cost_estimate=pl.CostEstimate(
            flops=4 * both * NB * tile_cols * (1 + later),
            bytes_accessed=4 * NB * tile_cols * (1 + later),
            transcendentals=0,
        ),
        name=f"stage{stage}",
    )(*operands)


def per_device(rhs, lower_factor, upper_factor, lower_rest, upper_rest, rest_solution, rest_rhs):
    rows, cols = lax.axis_size("row"), lax.axis_size("col")
    row_index = lax.axis_index("row")
    col_index = lax.axis_index("col")
    tile_rows = lower_factor.shape[1]
    tile_cols = lower_factor.shape[2]
    sources = rhs.shape[2]
    half = sources // rows
    both = 2 * half
    row_width = rows // BLOCKS
    width = cols // BLOCKS
    row_block = row_index // row_width
    col_block = col_index // width
    place = col_index % width
    bf16, f32 = jnp.bfloat16, jnp.float32

    tile = jnp.where(row_block >= col_block, lower_factor, upper_factor)
    tile = jnp.concatenate([tile[0], tile[1]], axis=1)
    lanes = 2 * tile_cols // tile_rows
    by_source = jnp.transpose(rhs, (0, 2, 1))
    by_source = by_source.reshape(2, lanes, AXIS_Y // lanes, AXIS_X, half, tile_rows)
    by_source = jnp.transpose(by_source, (3, 0, 2, 4, 1, 5)).reshape(AXIS_X, -1, 2 * tile_cols)
    near = exchange(jnp.concatenate([repeat_for(tile, AXIS_X), by_source], axis=1), "row", X_GROUPS)

    panel = lax.all_gather(
        near[:, :tile_rows].reshape(-1, 2 * tile_cols), "row", axis=0, tiled=True, axis_index_groups=Y_GROUPS
    )
    near_rhs = near[:, tile_rows:].reshape(AXIS_X, 2, AXIS_Y // lanes, half, lanes, tile_rows)
    near_rhs = jnp.transpose(near_rhs, (4, 2, 1, 3, 0, 5)).reshape(AXIS_Y, both, AXIS_X * tile_rows)
    near_rest = repeat_for(rest_solution.reshape(both, -1), AXIS_Y)
    sent = jnp.concatenate([near_rhs, near_rest], axis=2)
    upper = jnp.concatenate([upper_rest, upper_factor], axis=2)
    sent, upper = lax.optimization_barrier((sent, upper))
    got = exchange(sent, "row", Y_GROUPS)
    got, upper = lax.optimization_barrier((got, upper))
    wide_rows = AXIS_X * tile_rows
    per_block = AXIS_Y // BLOCKS
    own_rhs = lax.dynamic_slice_in_dim(got[..., :wide_rows], col_block * per_block, per_block, 0)
    own_rhs = jnp.transpose(own_rhs, (1, 0, 2)).reshape(both, NB).astype(f32)

    rest = got[..., wide_rows:].reshape(AXIS_Y, 2, half, -1)
    rest = jnp.transpose(rest, (1, 0, 2, 3)).reshape(2, AXIS_Y * half, -1)
    wide = exchange(repeat_for(upper, AXIS_X), "row", X_GROUPS)
    near_upper = wide[..., upper_rest.shape[2] :]
    near_upper = jnp.concatenate([near_upper[:, 0], near_upper[:, 1]], axis=2).reshape(-1, 2 * tile_cols)
    upper_panel = lax.all_gather(near_upper, "row", axis=0, tiled=True, axis_index_groups=Y_GROUPS)
    wide = jnp.transpose(wide[..., : upper_rest.shape[2]], (1, 0, 2, 3)).reshape(2, wide_rows, -1)
    real = nt(rest[0], wide[0]) - nt(rest[1], wide[1])
    imag = nt(rest[0], wide[1]) + nt(rest[1], wide[0])
    trailing = jnp.stack([real, imag]).astype(bf16).reshape(2, AXIS_Y, half, wide_rows)
    trailing = jnp.transpose(trailing, (1, 0, 2, 3)).reshape(AXIS_Y, both, wide_rows)
    trailing, own_rhs = lax.optimization_barrier((trailing, own_rhs))
    trailing = exchange(trailing, "row", Y_GROUPS)
    trailing = trailing.reshape(AXIS_Y, both, cols // AXIS_Y, tile_cols)
    trailing = jnp.transpose(trailing, (0, 2, 1, 3)).reshape(cols, both, tile_cols)
    trailing = jnp.sum(exchange(trailing, "col").astype(f32), axis=0)
    panel, trailing, own_rhs = lax.optimization_barrier((panel, trailing, own_rhs))

    where = jnp.stack([col_block, place]).astype(jnp.int32)

    def chain(sequence, start, diagonal, kept):
        extra = []
        for stage, k in enumerate(sequence):
            outs = run_stage(sequence, stage, width, where, start, kept, extra, diagonal, panel)
            kept = outs[0]
            if stage == len(sequence) - 1:
                return kept
            following = sequence[stage + 1]
            others = [j for j in sequence if j not in (k, following)]
            arrived = exchange(outs[1], "col", pair_groups((k, following), others, width))
            extra = [arrived, *outs[2:]]

    empty = jnp.zeros((both, tile_cols), bf16)
    forward = chain((0, 1, 2, 3), own_rhs, panel, empty)

    block_groups = [[k * width + i for i in range(width)] for k in range(BLOCKS)]
    base = repeat_for((forward.astype(f32) - trailing).astype(bf16), width)
    base, upper_panel = lax.optimization_barrier((base, upper_panel))
    upper_diagonal = lax.dynamic_slice_in_dim(upper_panel, col_block * NB, NB, 0)
    base, upper_diagonal = lax.optimization_barrier((base, upper_diagonal))
    base = exchange(base, "col", block_groups)
    base = jnp.transpose(base, (1, 0, 2)).reshape(both, NB).astype(f32)
    backward = chain((3, 2, 1, 0), base, upper_diagonal, empty)

    solved_all = exchange(repeat_for(jnp.concatenate([forward, backward], axis=1), rows), "row")
    solved_all = solved_all.reshape(rows, 2, half, 2 * tile_cols)
    forward_all = jnp.transpose(solved_all[..., :tile_cols], (1, 0, 2, 3)).reshape(2, sources, tile_cols)
    solution_rows = jnp.transpose(solved_all[..., tile_cols:], (1, 3, 0, 2))

    real = nt(lower_rest[0], forward_all[0]) - nt(lower_rest[1], forward_all[1])
    imag = nt(lower_rest[0], forward_all[1]) + nt(lower_rest[1], forward_all[0])
    update = jnp.stack([real, imag], axis=1).astype(bf16)
    update = exchange(update.reshape((cols, -1) + update.shape[1:]), "col")
    rest_out = rest_rhs.astype(f32) - jnp.sum(update.astype(f32), axis=0)
    return solution_rows.reshape(2, tile_cols, sources), rest_out.astype(bf16)


def solution(mesh):
    placed = (
        P(None, "row", None),
        P(None, "row", "col"),
        P(None, "row", "col"),
        P(None, "row", "col"),
        P(None, "row", "col"),
        P(None, "row", "col"),
        P(("row", "col"), None, None),
    )
    return jax.shard_map(
        per_device,
        mesh=mesh,
        in_specs=placed,
        out_specs=(P(None, "col", None), P(("row", "col"), None, None)),
        check_vma=False,
    )
```

```python
import functools

import jax
import jax.numpy as jnp
from jax import lax
from jax.experimental import pallas as pl
from jax.experimental.pallas import tpu as pltpu
from jax.sharding import PartitionSpec as P

N = 4096
NB = 1024
BLOCKS = N // NB
AXIS_Y, AXIS_X = 8, 4
X_GROUPS = [[y * AXIS_X + x for x in range(AXIS_X)] for y in range(AXIS_Y)]
Y_GROUPS = [[y * AXIS_X + x for y in range(AXIS_Y)] for x in range(AXIS_X)]


def nt(left, right):
    return lax.dot_general(left, right, (((1,), (1,)), ((), ())), preferred_element_type=jnp.float32)


def nn(left, right):
    return jnp.dot(left, right, preferred_element_type=jnp.float32)


def pair_groups(first, second, width):
    def members(k):
        return [k * width + i for i in range(width)]

    return [members(first[0]) + members(first[1]), members(second[0]) + members(second[1])]


def exchange(value, axis, groups=None):
    return lax.all_to_all(value, axis, 0, 0, axis_index_groups=groups)


def repeat_for(value, count):
    return jnp.broadcast_to(value[None], (count,) + value.shape)


def stage_kernel(sequence, stage, width, moving, *refs):
    k, later = sequence[stage], sequence[stage + 1 :]
    refs = list(refs)
    where, start, kept = refs[:3]
    rest = refs[3:]
    arrived = rest.pop(0) if stage else None
    before = rest.pop(0) if stage == 3 else None
    last_in = rest.pop(0) if stage == 1 else None
    diagonal = rest.pop(0)
    panel = rest.pop(0) if later else None
    kept_out = rest.pop(0)
    payload = rest.pop(0) if later else None
    reduced_out = rest.pop(0) if stage == 2 else None
    last_out = rest.pop(0) if stage == 0 else None
    diagonal_buf, diagonal_sem = rest.pop(0), rest.pop(0)
    bf16, f32 = jnp.bfloat16, jnp.float32
    block, place = where[0], where[1]

    first = pl.multiple_of(block * NB, NB) if moving else k * NB
    copy = pltpu.make_async_copy(diagonal.at[pl.ds(first, NB)], diagonal_buf, diagonal_sem)
    copy.start()
    panel_copies = []
    if later:
        panel_buf, panel_sem = rest.pop(0), rest.pop(0)
        for i, j in enumerate(later):
            panel_copies.append(
                pltpu.make_async_copy(panel.at[pl.ds(j * NB, NB)], panel_buf.at[i], panel_sem.at[i])
            )
            panel_copies[i].start()

    both = start.shape[0]
    half = both // 2
    tile_cols = kept.shape[1]
    residual = start[...]
    arrival = None
    if stage:
        arrival = arrived[0].astype(f32)
        for i in range(1, width):
            arrival = arrival + arrived[i].astype(f32)
        reduced = arrival[:, :NB]
        if stage == 3:
            reduced = reduced + before[...]
        if stage == 2:
            reduced_out[...] = reduced
        residual = residual - reduced
    residual = residual.astype(bf16)
    holder = block == k
    copy.wait()
    product = nn(residual, diagonal_buf[...])
    real = product[:half, :tile_cols] - product[half:, tile_cols:]
    imag = product[:half, tile_cols:] + product[half:, :tile_cols]
    value = jnp.concatenate([real, imag], axis=0).astype(bf16)
    kept_out[...] = jnp.where(holder, value, kept[...])
    if not later:
        return
    solved = jnp.where(holder, value, jnp.zeros_like(value)).astype(f32)
    real, imag = solved[:half], solved[half:]
    left = jnp.concatenate(
        [jnp.concatenate([real, -imag], axis=1), jnp.concatenate([imag, real], axis=1)], axis=0
    ).astype(bf16)
    panel_copies[0].wait()
    near = nt(left, panel_buf[0])
    carried = None
    if stage and arrival.shape[1] > NB:
        carried = arrival[:, NB:]
    for q in range(width):
        columns = slice(q * tile_cols, (q + 1) * tile_cols)
        piece = near[:, columns]
        if carried is not None:
            piece = piece + jnp.where(holder & (place == q), carried, 0.0)
        piece = piece.astype(bf16)
        if stage == 1:
            piece = jnp.where(block == sequence[0], last_in[:, columns], piece)
        for target in range(2 * width):
            payload[target, :, columns] = piece
    if len(later) > 1:
        panel_copies[1].wait()
        far = nt(left, panel_buf[1]).astype(bf16)
        for target in range(2 * width):
            q = target % width
            payload[target, :, NB:] = far[:, q * tile_cols : (q + 1) * tile_cols]
    if stage == 0:
        panel_copies[2].wait()
        last_out[...] = nt(left, panel_buf[2]).astype(bf16)


def run_stage(sequence, stage, width, moving, where, start, kept, extra, diagonal, panel):
    later = len(sequence) - 1 - stage
    both, tile_cols = kept.shape
    bf16, f32 = jnp.bfloat16, jnp.float32
    diagonal = pltpu.with_memory_space_constraint(diagonal, pltpu.HBM)
    operands = [where, start, kept, *extra, diagonal]
    vmem, anywhere = pl.BlockSpec(memory_space=pltpu.VMEM), pl.BlockSpec(memory_space=pl.ANY)
    in_specs = [pl.BlockSpec(memory_space=pltpu.SMEM)] + [vmem] * (2 + len(extra)) + [anywhere]
    out_shape = [jax.ShapeDtypeStruct(kept.shape, bf16)]
    scratch = [pltpu.VMEM((NB, 2 * tile_cols), bf16), pltpu.SemaphoreType.DMA]
    if later:
        operands.append(pltpu.with_memory_space_constraint(panel, pltpu.HBM))
        in_specs.append(anywhere)
        wide = NB + (tile_cols if later > 1 else 0)
        out_shape.append(jax.ShapeDtypeStruct((2 * width, both, wide), bf16))
        scratch += [pltpu.VMEM((later, NB, 2 * tile_cols), bf16), pltpu.SemaphoreType.DMA((later,))]
    if stage == 2:
        out_shape.append(jax.ShapeDtypeStruct((both, NB), f32))
    if stage == 0:
        out_shape.append(jax.ShapeDtypeStruct((both, NB), bf16))
    return pl.pallas_call(
        functools.partial(stage_kernel, sequence, stage, width, moving),
        out_shape=out_shape,
        in_specs=in_specs,
        out_specs=[vmem] * len(out_shape),
        scratch_shapes=scratch,
        compiler_params=pltpu.CompilerParams(vmem_limit_bytes=14 * 2**20),
        cost_estimate=pl.CostEstimate(
            flops=4 * both * NB * tile_cols * (1 + later),
            bytes_accessed=4 * NB * tile_cols * (1 + later),
            transcendentals=0,
        ),
        name=f"stage{stage}",
    )(*operands)


def per_device(rhs, lower_factor, upper_factor, lower_rest, upper_rest, rest_solution, rest_rhs):
    rows, cols = lax.axis_size("row"), lax.axis_size("col")
    row_index = lax.axis_index("row")
    col_index = lax.axis_index("col")
    tile_rows = lower_factor.shape[1]
    tile_cols = lower_factor.shape[2]
    sources = rhs.shape[2]
    half = sources // rows
    both = 2 * half
    row_width = rows // BLOCKS
    width = cols // BLOCKS
    row_block = row_index // row_width
    col_block = col_index // width
    place = col_index % width
    bf16, f32 = jnp.bfloat16, jnp.float32

    tile = jnp.where(row_block >= col_block, lower_factor, upper_factor)
    tile = jnp.concatenate([tile[0], tile[1]], axis=1)
    lanes = 2 * tile_cols // tile_rows
    by_source = jnp.transpose(rhs, (0, 2, 1))
    by_source = by_source.reshape(2, lanes, AXIS_Y // lanes, AXIS_X, half, tile_rows)
    by_source = jnp.transpose(by_source, (3, 0, 2, 4, 1, 5)).reshape(AXIS_X, -1, 2 * tile_cols)
    near = exchange(jnp.concatenate([repeat_for(tile, AXIS_X), by_source], axis=1), "row", X_GROUPS)

    panel = lax.all_gather(
        near[:, :tile_rows].reshape(-1, 2 * tile_cols), "row", axis=0, tiled=True, axis_index_groups=Y_GROUPS
    )
    near_rhs = near[:, tile_rows:].reshape(AXIS_X, 2, AXIS_Y // lanes, half, lanes, tile_rows)
    near_rhs = jnp.transpose(near_rhs, (4, 2, 1, 3, 0, 5)).reshape(AXIS_Y, both, AXIS_X * tile_rows)
    near_rest = repeat_for(rest_solution.reshape(both, -1), AXIS_Y)
    sent = jnp.concatenate([near_rhs, near_rest], axis=2)
    upper = jnp.concatenate([upper_rest, upper_factor], axis=2)
    sent, upper = lax.optimization_barrier((sent, upper))
    got = exchange(sent, "row", Y_GROUPS)
    got, upper = lax.optimization_barrier((got, upper))
    wide_rows = AXIS_X * tile_rows
    per_block = AXIS_Y // BLOCKS
    own_rhs = lax.dynamic_slice_in_dim(got[..., :wide_rows], col_block * per_block, per_block, 0)
    own_rhs = jnp.transpose(own_rhs, (1, 0, 2)).reshape(both, NB).astype(f32)

    rest = got[..., wide_rows:].reshape(AXIS_Y, 2, half, -1)
    rest = jnp.transpose(rest, (1, 0, 2, 3)).reshape(2, AXIS_Y * half, -1)
    wide = exchange(repeat_for(upper, AXIS_X), "row", X_GROUPS)
    near_upper = wide[..., upper_rest.shape[2] :]
    near_upper = jnp.concatenate([near_upper[:, 0], near_upper[:, 1]], axis=2).reshape(-1, 2 * tile_cols)
    upper_panel = lax.all_gather(near_upper, "row", axis=0, tiled=True, axis_index_groups=Y_GROUPS)
    wide = jnp.transpose(wide[..., : upper_rest.shape[2]], (1, 0, 2, 3)).reshape(2, wide_rows, -1)
    real = nt(rest[0], wide[0]) - nt(rest[1], wide[1])
    imag = nt(rest[0], wide[1]) + nt(rest[1], wide[0])
    trailing = jnp.stack([real, imag]).astype(bf16).reshape(2, AXIS_Y, half, wide_rows)
    trailing = jnp.transpose(trailing, (1, 0, 2, 3)).reshape(AXIS_Y, both, wide_rows)
    trailing, own_rhs = lax.optimization_barrier((trailing, own_rhs))
    trailing = exchange(trailing, "row", Y_GROUPS)
    trailing = trailing.reshape(AXIS_Y, both, cols // AXIS_Y, tile_cols)
    trailing = jnp.transpose(trailing, (0, 2, 1, 3)).reshape(cols, both, tile_cols)
    trailing = jnp.sum(exchange(trailing, "col").astype(f32), axis=0)
    panel, trailing, own_rhs = lax.optimization_barrier((panel, trailing, own_rhs))

    where = jnp.stack([col_block, place]).astype(jnp.int32)

    def chain(sequence, start, diagonal, moving, kept):
        extra = []
        for stage, k in enumerate(sequence):
            outs = run_stage(sequence, stage, width, moving, where, start, kept, extra, diagonal, panel)
            kept = outs[0]
            if stage == len(sequence) - 1:
                return kept
            following = sequence[stage + 1]
            others = [j for j in sequence if j not in (k, following)]
            arrived = exchange(outs[1], "col", pair_groups((k, following), others, width))
            extra = [arrived, *outs[2:]]

    empty = jnp.zeros((both, tile_cols), bf16)
    forward = chain((0, 1, 2, 3), own_rhs, panel, False, empty)

    block_groups = [[k * width + i for i in range(width)] for k in range(BLOCKS)]
    base = repeat_for((forward.astype(f32) - trailing).astype(bf16), width)
    base = exchange(base, "col", block_groups)
    base = jnp.transpose(base, (1, 0, 2)).reshape(both, NB).astype(f32)
    backward = chain((3, 2, 1, 0), base, upper_panel, True, empty)

    solved_all = exchange(repeat_for(jnp.concatenate([forward, backward], axis=1), rows), "row")
    solved_all = solved_all.reshape(rows, 2, half, 2 * tile_cols)
    forward_all = jnp.transpose(solved_all[..., :tile_cols], (1, 0, 2, 3)).reshape(2, sources, tile_cols)
    solution_rows = jnp.transpose(solved_all[..., tile_cols:], (1, 3, 0, 2))

    real = nt(lower_rest[0], forward_all[0]) - nt(lower_rest[1], forward_all[1])
    imag = nt(lower_rest[0], forward_all[1]) + nt(lower_rest[1], forward_all[0])
    update = jnp.stack([real, imag], axis=1).astype(bf16)
    update = exchange(update.reshape((cols, -1) + update.shape[1:]), "col")
    rest_out = rest_rhs.astype(f32) - jnp.sum(update.astype(f32), axis=0)
    return solution_rows.reshape(2, tile_cols, sources), rest_out.astype(bf16)


def solution(mesh):
    placed = (
        P(None, "row", None),
        P(None, "row", "col"),
        P(None, "row", "col"),
        P(None, "row", "col"),
        P(None, "row", "col"),
        P(None, "row", "col"),
        P(("row", "col"), None, None),
    )
    return jax.shard_map(
        per_device,
        mesh=mesh,
        in_specs=placed,
        out_specs=(P(None, "col", None), P(("row", "col"), None, None)),
        check_vma=False,
    )
```

```python
import functools

import jax
import jax.numpy as jnp
from jax import lax
from jax.experimental import pallas as pl
from jax.experimental.pallas import tpu as pltpu
from jax.sharding import PartitionSpec as P

N = 4096
NB = 1024
BLOCKS = N // NB
CHUNKS = 4
AXIS_Y, AXIS_X = 8, 4
X_GROUPS = [[y * AXIS_X + x for x in range(AXIS_X)] for y in range(AXIS_Y)]
Y_GROUPS = [[y * AXIS_X + x for y in range(AXIS_Y)] for x in range(AXIS_X)]


def nt(left, right):
    return lax.dot_general(left, right, (((1,), (1,)), ((), ())), preferred_element_type=jnp.float32)


def nn(left, right):
    return jnp.dot(left, right, preferred_element_type=jnp.float32)


def pair_groups(first, second, width):
    def members(k):
        return [k * width + i for i in range(width)]

    return [members(first[0]) + members(first[1]), members(second[0]) + members(second[1])]


def exchange(value, axis, groups=None):
    return lax.all_to_all(value, axis, 0, 0, axis_index_groups=groups)


def repeat_for(value, count):
    return jnp.broadcast_to(value[None], (count,) + value.shape)


def stage_kernel(sequence, stage, width, moving, *refs):
    k, later = sequence[stage], sequence[stage + 1 :]
    refs = list(refs)
    where, start, kept = refs[:3]
    rest = refs[3:]
    arrived = rest.pop(0) if stage else None
    before = rest.pop(0) if stage == 3 else None
    last_in = rest.pop(0) if stage == 1 else None
    diagonal = rest.pop(0)
    panel = rest.pop(0) if later else None
    kept_out = rest.pop(0)
    payload = rest.pop(0) if later else None
    reduced_out = rest.pop(0) if stage == 2 else None
    last_out = rest.pop(0) if stage == 0 else None
    diagonal_buf, diagonal_sem = rest.pop(0), rest.pop(0)
    bf16, f32 = jnp.bfloat16, jnp.float32
    block, place = where[0], where[1]

    chunk = NB // CHUNKS
    copies, panel_copies = [], []
    for c in range(CHUNKS):
        first = pl.multiple_of(block * NB, NB) + c * chunk if moving else k * NB + c * chunk
        if moving:
            first = pl.multiple_of(first, chunk)
        copies.append(
            pltpu.make_async_copy(
                diagonal.at[pl.ds(first, chunk)], diagonal_buf.at[pl.ds(c * chunk, chunk)], diagonal_sem.at[c]
            )
        )
        copies[c].start()
    if later:
        panel_buf, panel_sem = rest.pop(0), rest.pop(0)
        for i, j in enumerate(later):
            panel_copies.append([])
            for c in range(CHUNKS):
                part = pltpu.make_async_copy(
                    panel.at[pl.ds(j * NB + c * chunk, chunk)],
                    panel_buf.at[i, pl.ds(c * chunk, chunk)],
                    panel_sem.at[i, c],
                )
                part.start()
                panel_copies[i].append(part)

    both = start.shape[0]
    half = both // 2
    tile_cols = kept.shape[1]
    residual = start[...]
    arrival = None
    if stage:
        arrival = arrived[0].astype(f32)
        for i in range(1, width):
            arrival = arrival + arrived[i].astype(f32)
        reduced = arrival[:, :NB]
        if stage == 3:
            reduced = reduced + before[...]
        if stage == 2:
            reduced_out[...] = reduced
        residual = residual - reduced
    residual = residual.astype(bf16)
    holder = block == k
    product = None
    for c in range(CHUNKS):
        copies[c].wait()
        span = slice(c * chunk, (c + 1) * chunk)
        part = nn(residual[:, span], diagonal_buf[span])
        product = part if product is None else product + part
    real = product[:half, :tile_cols] - product[half:, tile_cols:]
    imag = product[:half, tile_cols:] + product[half:, :tile_cols]
    value = jnp.concatenate([real, imag], axis=0).astype(bf16)
    kept_out[...] = jnp.where(holder, value, kept[...])
    if not later:
        return
    solved = jnp.where(holder, value, jnp.zeros_like(value)).astype(f32)
    real, imag = solved[:half], solved[half:]
    left = jnp.concatenate(
        [jnp.concatenate([real, -imag], axis=1), jnp.concatenate([imag, real], axis=1)], axis=0
    ).astype(bf16)

    def later_product(i):
        pieces = []
        for c in range(CHUNKS):
            panel_copies[i][c].wait()
            pieces.append(nt(left, panel_buf[i, c * chunk : (c + 1) * chunk]))
        return jnp.concatenate(pieces, axis=1)

    near = later_product(0)
    carried = None
    if stage and arrival.shape[1] > NB:
        carried = arrival[:, NB:]
    for q in range(width):
        columns = slice(q * tile_cols, (q + 1) * tile_cols)
        piece = near[:, columns]
        if carried is not None:
            piece = piece + jnp.where(holder & (place == q), carried, 0.0)
        piece = piece.astype(bf16)
        if stage == 1:
            piece = jnp.where(block == sequence[0], last_in[:, columns], piece)
        for target in range(2 * width):
            payload[target, :, columns] = piece
    if len(later) > 1:
        far = later_product(1).astype(bf16)
        for target in range(2 * width):
            q = target % width
            payload[target, :, NB:] = far[:, q * tile_cols : (q + 1) * tile_cols]
    if stage == 0:
        last_out[...] = later_product(2).astype(bf16)


def run_stage(sequence, stage, width, moving, where, start, kept, extra, diagonal, panel):
    later = len(sequence) - 1 - stage
    both, tile_cols = kept.shape
    bf16, f32 = jnp.bfloat16, jnp.float32
    diagonal = pltpu.with_memory_space_constraint(diagonal, pltpu.HBM)
    operands = [where, start, kept, *extra, diagonal]
    vmem, anywhere = pl.BlockSpec(memory_space=pltpu.VMEM), pl.BlockSpec(memory_space=pl.ANY)
    in_specs = [pl.BlockSpec(memory_space=pltpu.SMEM)] + [vmem] * (2 + len(extra)) + [anywhere]
    out_shape = [jax.ShapeDtypeStruct(kept.shape, bf16)]
    scratch = [pltpu.VMEM((NB, 2 * tile_cols), bf16), pltpu.SemaphoreType.DMA((CHUNKS,))]
    if later:
        operands.append(pltpu.with_memory_space_constraint(panel, pltpu.HBM))
        in_specs.append(anywhere)
        wide = NB + (tile_cols if later > 1 else 0)
        out_shape.append(jax.ShapeDtypeStruct((2 * width, both, wide), bf16))
        scratch += [pltpu.VMEM((later, NB, 2 * tile_cols), bf16), pltpu.SemaphoreType.DMA((later, CHUNKS))]
    if stage == 2:
        out_shape.append(jax.ShapeDtypeStruct((both, NB), f32))
    if stage == 0:
        out_shape.append(jax.ShapeDtypeStruct((both, NB), bf16))
    return pl.pallas_call(
        functools.partial(stage_kernel, sequence, stage, width, moving),
        out_shape=out_shape,
        in_specs=in_specs,
        out_specs=[vmem] * len(out_shape),
        scratch_shapes=scratch,
        compiler_params=pltpu.CompilerParams(vmem_limit_bytes=14 * 2**20),
        cost_estimate=pl.CostEstimate(
            flops=4 * both * NB * tile_cols * (1 + later),
            bytes_accessed=4 * NB * tile_cols * (1 + later),
            transcendentals=0,
        ),
        name=f"stage{stage}",
    )(*operands)


def per_device(rhs, lower_factor, upper_factor, lower_rest, upper_rest, rest_solution, rest_rhs):
    rows, cols = lax.axis_size("row"), lax.axis_size("col")
    row_index = lax.axis_index("row")
    col_index = lax.axis_index("col")
    tile_rows = lower_factor.shape[1]
    tile_cols = lower_factor.shape[2]
    sources = rhs.shape[2]
    half = sources // rows
    both = 2 * half
    row_width = rows // BLOCKS
    width = cols // BLOCKS
    row_block = row_index // row_width
    col_block = col_index // width
    place = col_index % width
    bf16, f32 = jnp.bfloat16, jnp.float32

    tile = jnp.where(row_block >= col_block, lower_factor, upper_factor)
    tile = jnp.concatenate([tile[0], tile[1]], axis=1)
    lanes = 2 * tile_cols // tile_rows
    by_source = jnp.transpose(rhs, (0, 2, 1))
    by_source = by_source.reshape(2, lanes, AXIS_Y // lanes, AXIS_X, half, tile_rows)
    by_source = jnp.transpose(by_source, (3, 0, 2, 4, 1, 5)).reshape(AXIS_X, -1, 2 * tile_cols)
    near = exchange(jnp.concatenate([repeat_for(tile, AXIS_X), by_source], axis=1), "row", X_GROUPS)

    panel = lax.all_gather(
        near[:, :tile_rows].reshape(-1, 2 * tile_cols), "row", axis=0, tiled=True, axis_index_groups=Y_GROUPS
    )
    near_rhs = near[:, tile_rows:].reshape(AXIS_X, 2, AXIS_Y // lanes, half, lanes, tile_rows)
    near_rhs = jnp.transpose(near_rhs, (4, 2, 1, 3, 0, 5)).reshape(AXIS_Y, both, AXIS_X * tile_rows)
    near_rest = repeat_for(rest_solution.reshape(both, -1), AXIS_Y)
    sent = jnp.concatenate([near_rhs, near_rest], axis=2)
    upper = jnp.concatenate([upper_rest, upper_factor], axis=2)
    sent, upper = lax.optimization_barrier((sent, upper))
    got = exchange(sent, "row", Y_GROUPS)
    got, upper = lax.optimization_barrier((got, upper))
    wide_rows = AXIS_X * tile_rows
    per_block = AXIS_Y // BLOCKS
    own_rhs = lax.dynamic_slice_in_dim(got[..., :wide_rows], col_block * per_block, per_block, 0)
    own_rhs = jnp.transpose(own_rhs, (1, 0, 2)).reshape(both, NB).astype(f32)

    rest = got[..., wide_rows:].reshape(AXIS_Y, 2, half, -1)
    rest = jnp.transpose(rest, (1, 0, 2, 3)).reshape(2, AXIS_Y * half, -1)
    wide = exchange(repeat_for(upper, AXIS_X), "row", X_GROUPS)
    near_upper = wide[..., upper_rest.shape[2] :]
    near_upper = jnp.concatenate([near_upper[:, 0], near_upper[:, 1]], axis=2).reshape(-1, 2 * tile_cols)
    upper_panel = lax.all_gather(near_upper, "row", axis=0, tiled=True, axis_index_groups=Y_GROUPS)
    wide = jnp.transpose(wide[..., : upper_rest.shape[2]], (1, 0, 2, 3)).reshape(2, wide_rows, -1)
    real = nt(rest[0], wide[0]) - nt(rest[1], wide[1])
    imag = nt(rest[0], wide[1]) + nt(rest[1], wide[0])
    trailing = jnp.stack([real, imag]).astype(bf16).reshape(2, AXIS_Y, half, wide_rows)
    trailing = jnp.transpose(trailing, (1, 0, 2, 3)).reshape(AXIS_Y, both, wide_rows)
    trailing, own_rhs = lax.optimization_barrier((trailing, own_rhs))
    trailing = exchange(trailing, "row", Y_GROUPS)
    trailing = trailing.reshape(AXIS_Y, both, cols // AXIS_Y, tile_cols)
    trailing = jnp.transpose(trailing, (0, 2, 1, 3)).reshape(cols, both, tile_cols)
    trailing = jnp.sum(exchange(trailing, "col").astype(f32), axis=0)
    panel, trailing, own_rhs = lax.optimization_barrier((panel, trailing, own_rhs))

    where = jnp.stack([col_block, place]).astype(jnp.int32)

    def chain(sequence, start, diagonal, moving, kept):
        extra = []
        for stage, k in enumerate(sequence):
            outs = run_stage(sequence, stage, width, moving, where, start, kept, extra, diagonal, panel)
            kept = outs[0]
            if stage == len(sequence) - 1:
                return kept
            following = sequence[stage + 1]
            others = [j for j in sequence if j not in (k, following)]
            arrived = exchange(outs[1], "col", pair_groups((k, following), others, width))
            extra = [arrived, *outs[2:]]

    empty = jnp.zeros((both, tile_cols), bf16)
    forward = chain((0, 1, 2, 3), own_rhs, panel, False, empty)

    block_groups = [[k * width + i for i in range(width)] for k in range(BLOCKS)]
    base = repeat_for((forward.astype(f32) - trailing).astype(bf16), width)
    base = exchange(base, "col", block_groups)
    base = jnp.transpose(base, (1, 0, 2)).reshape(both, NB).astype(f32)
    backward = chain((3, 2, 1, 0), base, upper_panel, True, empty)

    solved_all = exchange(repeat_for(jnp.concatenate([forward, backward], axis=1), rows), "row")
    solved_all = solved_all.reshape(rows, 2, half, 2 * tile_cols)
    forward_all = jnp.transpose(solved_all[..., :tile_cols], (1, 0, 2, 3)).reshape(2, sources, tile_cols)
    solution_rows = jnp.transpose(solved_all[..., tile_cols:], (1, 3, 0, 2))

    real = nt(lower_rest[0], forward_all[0]) - nt(lower_rest[1], forward_all[1])
    imag = nt(lower_rest[0], forward_all[1]) + nt(lower_rest[1], forward_all[0])
    update = jnp.stack([real, imag], axis=1).astype(bf16)
    update = exchange(update.reshape((cols, -1) + update.shape[1:]), "col")
    rest_out = rest_rhs.astype(f32) - jnp.sum(update.astype(f32), axis=0)
    return solution_rows.reshape(2, tile_cols, sources), rest_out.astype(bf16)


def solution(mesh):
    placed = (
        P(None, "row", None),
        P(None, "row", "col"),
        P(None, "row", "col"),
        P(None, "row", "col"),
        P(None, "row", "col"),
        P(None, "row", "col"),
        P(("row", "col"), None, None),
    )
    return jax.shard_map(
        per_device,
        mesh=mesh,
        in_specs=placed,
        out_specs=(P(None, "col", None), P(("row", "col"), None, None)),
        check_vma=False,
    )
```

```python
import functools

import jax
import jax.numpy as jnp
from jax import lax
from jax.experimental import pallas as pl
from jax.experimental.pallas import tpu as pltpu
from jax.sharding import PartitionSpec as P

N = 4096
NB = 1024
BLOCKS = N // NB
AXIS_Y, AXIS_X = 8, 4
X_GROUPS = [[y * AXIS_X + x for x in range(AXIS_X)] for y in range(AXIS_Y)]
Y_GROUPS = [[y * AXIS_X + x for y in range(AXIS_Y)] for x in range(AXIS_X)]


def nt(left, right):
    return lax.dot_general(left, right, (((1,), (1,)), ((), ())), preferred_element_type=jnp.float32)


def nn(left, right):
    return jnp.dot(left, right, preferred_element_type=jnp.float32)


def pair_groups(first, second, width):
    def members(k):
        return [k * width + i for i in range(width)]

    return [members(first[0]) + members(first[1]), members(second[0]) + members(second[1])]


def exchange(value, axis, groups=None):
    return lax.all_to_all(value, axis, 0, 0, axis_index_groups=groups)


def repeat_for(value, count):
    return jnp.broadcast_to(value[None], (count,) + value.shape)


def stage_kernel(sequence, stage, width, *refs):
    k, later = sequence[stage], sequence[stage + 1 :]
    refs = list(refs)
    where, start, kept = refs[:3]
    rest = refs[3:]
    arrived = rest.pop(0) if stage else None
    before = rest.pop(0) if stage == 3 else None
    last_in = rest.pop(0) if stage == 1 else None
    diagonal = rest.pop(0)
    panel = rest.pop(0) if later else None
    kept_out = rest.pop(0)
    payload = rest.pop(0) if later else None
    reduced_out = rest.pop(0) if stage == 2 else None
    last_out = rest.pop(0) if stage == 0 else None
    diagonal_buf, diagonal_sem = rest.pop(0), rest.pop(0)
    bf16, f32 = jnp.bfloat16, jnp.float32
    block, place = where[0], where[1]

    first = 0 if diagonal.shape[0] == NB else k * NB
    copy = pltpu.make_async_copy(diagonal.at[pl.ds(first, NB)], diagonal_buf, diagonal_sem)
    copy.start()
    panel_copies = []
    if later:
        panel_buf, panel_sem = rest.pop(0), rest.pop(0)
        for i, j in enumerate(later):
            panel_copies.append(
                pltpu.make_async_copy(panel.at[pl.ds(j * NB, NB)], panel_buf.at[i], panel_sem.at[i])
            )
            panel_copies[i].start()

    both = start.shape[0]
    half = both // 2
    tile_cols = kept.shape[1]
    residual = start[...]
    arrival = None
    if stage:
        arrival = arrived[0].astype(f32)
        for i in range(1, width):
            arrival = arrival + arrived[i].astype(f32)
        reduced = arrival[:, :NB]
        if stage == 3:
            reduced = reduced + before[...]
        if stage == 2:
            reduced_out[...] = reduced
        residual = residual - reduced
    residual = residual.astype(bf16)
    holder = block == k
    copy.wait()
    product = nn(residual, diagonal_buf[...])
    real = product[:half, :tile_cols] - product[half:, tile_cols:]
    imag = product[:half, tile_cols:] + product[half:, :tile_cols]
    value = jnp.concatenate([real, imag], axis=0).astype(bf16)
    kept_out[...] = jnp.where(holder, value, kept[...])
    if not later:
        return
    solved = jnp.where(holder, value, jnp.zeros_like(value)).astype(f32)
    real, imag = solved[:half], solved[half:]
    left = jnp.concatenate(
        [jnp.concatenate([real, -imag], axis=1), jnp.concatenate([imag, real], axis=1)], axis=0
    ).astype(bf16)
    panel_copies[0].wait()
    near = nt(left, panel_buf[0])
    carried = None
    if stage and arrival.shape[1] > NB:
        carried = arrival[:, NB:]
    for q in range(width):
        columns = slice(q * tile_cols, (q + 1) * tile_cols)
        piece = near[:, columns]
        if carried is not None:
            piece = piece + jnp.where(holder & (place == q), carried, 0.0)
        piece = piece.astype(bf16)
        if stage == 1:
            piece = jnp.where(block == sequence[0], last_in[:, columns], piece)
        for target in range(2 * width):
            payload[target, :, columns] = piece
    if len(later) > 1:
        panel_copies[1].wait()
        far = nt(left, panel_buf[1]).astype(bf16)
        for target in range(2 * width):
            q = target % width
            payload[target, :, NB:] = far[:, q * tile_cols : (q + 1) * tile_cols]
    if stage == 0:
        panel_copies[2].wait()
        last_out[...] = nt(left, panel_buf[2]).astype(bf16)


def run_stage(sequence, stage, width, where, start, kept, extra, diagonal, panel):
    later = len(sequence) - 1 - stage
    both, tile_cols = kept.shape
    bf16, f32 = jnp.bfloat16, jnp.float32
    if stage in (0, 3) and diagonal.shape[0] > NB:
        diagonal = pltpu.with_memory_space_constraint(diagonal, pltpu.HBM)
    operands = [where, start, kept, *extra, diagonal]
    vmem, anywhere = pl.BlockSpec(memory_space=pltpu.VMEM), pl.BlockSpec(memory_space=pl.ANY)
    in_specs = [pl.BlockSpec(memory_space=pltpu.SMEM)] + [vmem] * (2 + len(extra)) + [anywhere]
    out_shape = [jax.ShapeDtypeStruct(kept.shape, bf16)]
    scratch = [pltpu.VMEM((NB, 2 * tile_cols), bf16), pltpu.SemaphoreType.DMA]
    if later:
        operands.append(panel if stage else pltpu.with_memory_space_constraint(panel, pltpu.HBM))
        in_specs.append(anywhere)
        wide = NB + (tile_cols if later > 1 else 0)
        out_shape.append(jax.ShapeDtypeStruct((2 * width, both, wide), bf16))
        scratch += [pltpu.VMEM((later, NB, 2 * tile_cols), bf16), pltpu.SemaphoreType.DMA((later,))]
    if stage == 2:
        out_shape.append(jax.ShapeDtypeStruct((both, NB), f32))
    if stage == 0:
        out_shape.append(jax.ShapeDtypeStruct((both, NB), bf16))
    return pl.pallas_call(
        functools.partial(stage_kernel, sequence, stage, width),
        out_shape=out_shape,
        in_specs=in_specs,
        out_specs=[vmem] * len(out_shape),
        scratch_shapes=scratch,
        compiler_params=pltpu.CompilerParams(vmem_limit_bytes=14 * 2**20),
        cost_estimate=pl.CostEstimate(
            flops=4 * both * NB * tile_cols * (1 + later),
            bytes_accessed=4 * NB * tile_cols * (1 + later),
            transcendentals=0,
        ),
        name=f"stage{stage}",
    )(*operands)


def per_device(rhs, lower_factor, upper_factor, lower_rest, upper_rest, rest_solution, rest_rhs):
    rows, cols = lax.axis_size("row"), lax.axis_size("col")
    row_index = lax.axis_index("row")
    col_index = lax.axis_index("col")
    tile_rows = lower_factor.shape[1]
    tile_cols = lower_factor.shape[2]
    sources = rhs.shape[2]
    half = sources // rows
    both = 2 * half
    row_width = rows // BLOCKS
    width = cols // BLOCKS
    row_block = row_index // row_width
    col_block = col_index // width
    place = col_index % width
    bf16, f32 = jnp.bfloat16, jnp.float32

    tile = jnp.where(row_block >= col_block, lower_factor, upper_factor)
    tile = jnp.concatenate([tile[0], tile[1]], axis=1)
    lanes = 2 * tile_cols // tile_rows
    by_source = jnp.transpose(rhs, (0, 2, 1))
    by_source = by_source.reshape(2, lanes, AXIS_Y // lanes, AXIS_X, half, tile_rows)
    by_source = jnp.transpose(by_source, (3, 0, 2, 4, 1, 5)).reshape(AXIS_X, -1, 2 * tile_cols)
    near = exchange(jnp.concatenate([repeat_for(tile, AXIS_X), by_source], axis=1), "row", X_GROUPS)

    panel = lax.all_gather(
        near[:, :tile_rows].reshape(-1, 2 * tile_cols), "row", axis=0, tiled=True, axis_index_groups=Y_GROUPS
    )
    near_rhs = near[:, tile_rows:].reshape(AXIS_X, 2, AXIS_Y // lanes, half, lanes, tile_rows)
    near_rhs = jnp.transpose(near_rhs, (4, 2, 1, 3, 0, 5)).reshape(AXIS_Y, both, AXIS_X * tile_rows)
    near_rest = repeat_for(rest_solution.reshape(both, -1), AXIS_Y)
    sent = jnp.concatenate([near_rhs, near_rest], axis=2)
    upper = jnp.concatenate([upper_rest, upper_factor], axis=2)
    sent, upper = lax.optimization_barrier((sent, upper))
    got = exchange(sent, "row", Y_GROUPS)
    got, upper = lax.optimization_barrier((got, upper))
    wide_rows = AXIS_X * tile_rows
    per_block = AXIS_Y // BLOCKS
    own_rhs = lax.dynamic_slice_in_dim(got[..., :wide_rows], col_block * per_block, per_block, 0)
    own_rhs = jnp.transpose(own_rhs, (1, 0, 2)).reshape(both, NB).astype(f32)

    rest = got[..., wide_rows:].reshape(AXIS_Y, 2, half, -1)
    rest = jnp.transpose(rest, (1, 0, 2, 3)).reshape(2, AXIS_Y * half, -1)
    wide = exchange(repeat_for(upper, AXIS_X), "row", X_GROUPS)
    near_upper = wide[..., upper_rest.shape[2] :]
    near_upper = jnp.concatenate([near_upper[:, 0], near_upper[:, 1]], axis=2).reshape(-1, 2 * tile_cols)
    upper_panel = lax.all_gather(near_upper, "row", axis=0, tiled=True, axis_index_groups=Y_GROUPS)
    wide = jnp.transpose(wide[..., : upper_rest.shape[2]], (1, 0, 2, 3)).reshape(2, wide_rows, -1)
    real = nt(rest[0], wide[0]) - nt(rest[1], wide[1])
    imag = nt(rest[0], wide[1]) + nt(rest[1], wide[0])
    trailing = jnp.stack([real, imag]).astype(bf16).reshape(2, AXIS_Y, half, wide_rows)
    trailing = jnp.transpose(trailing, (1, 0, 2, 3)).reshape(AXIS_Y, both, wide_rows)
    trailing, own_rhs = lax.optimization_barrier((trailing, own_rhs))
    trailing = exchange(trailing, "row", Y_GROUPS)
    trailing = trailing.reshape(AXIS_Y, both, cols // AXIS_Y, tile_cols)
    trailing = jnp.transpose(trailing, (0, 2, 1, 3)).reshape(cols, both, tile_cols)
    trailing = jnp.sum(exchange(trailing, "col").astype(f32), axis=0)
    panel, trailing, own_rhs = lax.optimization_barrier((panel, trailing, own_rhs))

    where = jnp.stack([col_block, place]).astype(jnp.int32)

    def chain(sequence, start, diagonal, kept):
        extra = []
        for stage, k in enumerate(sequence):
            outs = run_stage(sequence, stage, width, where, start, kept, extra, diagonal, panel)
            kept = outs[0]
            if stage == len(sequence) - 1:
                return kept
            following = sequence[stage + 1]
            others = [j for j in sequence if j not in (k, following)]
            arrived = exchange(outs[1], "col", pair_groups((k, following), others, width))
            extra = [arrived, *outs[2:]]

    empty = jnp.zeros((both, tile_cols), bf16)
    forward = chain((0, 1, 2, 3), own_rhs, panel, empty)

    block_groups = [[k * width + i for i in range(width)] for k in range(BLOCKS)]
    base = repeat_for((forward.astype(f32) - trailing).astype(bf16), width)
    base, upper_panel = lax.optimization_barrier((base, upper_panel))
    upper_diagonal = lax.dynamic_slice_in_dim(upper_panel, col_block * NB, NB, 0)
    base, upper_diagonal = lax.optimization_barrier((base, upper_diagonal))
    base = exchange(base, "col", block_groups)
    base = jnp.transpose(base, (1, 0, 2)).reshape(both, NB).astype(f32)
    backward = chain((3, 2, 1, 0), base, upper_diagonal, empty)

    solved_all = exchange(repeat_for(jnp.concatenate([forward, backward], axis=1), rows), "row")
    solved_all = solved_all.reshape(rows, 2, half, 2 * tile_cols)
    forward_all = jnp.transpose(solved_all[..., :tile_cols], (1, 0, 2, 3)).reshape(2, sources, tile_cols)
    solution_rows = jnp.transpose(solved_all[..., tile_cols:], (1, 3, 0, 2))

    real = nt(lower_rest[0], forward_all[0]) - nt(lower_rest[1], forward_all[1])
    imag = nt(lower_rest[0], forward_all[1]) + nt(lower_rest[1], forward_all[0])
    update = jnp.stack([real, imag], axis=1).astype(bf16)
    update = exchange(update.reshape((cols, -1) + update.shape[1:]), "col")
    rest_out = rest_rhs.astype(f32) - jnp.sum(update.astype(f32), axis=0)
    return solution_rows.reshape(2, tile_cols, sources), rest_out.astype(bf16)


def solution(mesh):
    placed = (
        P(None, "row", None),
        P(None, "row", "col"),
        P(None, "row", "col"),
        P(None, "row", "col"),
        P(None, "row", "col"),
        P(None, "row", "col"),
        P(("row", "col"), None, None),
    )
    return jax.shard_map(
        per_device,
        mesh=mesh,
        in_specs=placed,
        out_specs=(P(None, "col", None), P(("row", "col"), None, None)),
        check_vma=False,
    )
```
